256 devices in a mesh: rep: 8 (over z_lo, core), shard: 32 (over x, z_hi, y).
Axes of the slice: x: 4, y: 4, z: 8 (z_hi: 2, z_lo: 4; z = z_hi * 4 + z_lo), core: 2. Of those that a mesh axis runs over, the one named last changes fastest.
Arguments:
- grad: bfloat16 [8, 512, 131072], P('rep', 'shard'), may hold values from -6 to 6
- owner_rep: int32 [32, 8], replicated, may hold values from 0 to 7, each once within a row
- stat_left: float32 [256, 512, 512], P(('rep', 'shard')), may hold values from -4 to 4
- stat_right: float32 [256, 512, 512], P(('rep', 'shard')), may hold values from -4 to 4
- root_left: bfloat16 [256, 512, 512], P(('rep', 'shard')), may hold values from -1 to 5
- root_right: bfloat16 [256, 512, 512], P(('rep', 'shard')), may hold values from -1 to 5
Outputs:
- new_left: float32 [256, 512, 512], P(('rep', 'shard'))
- new_right: float32 [256, 512, 512], P(('rep', 'shard'))
- update: bfloat16 [512, 131072], P('shard')
The draws below stay inside these ranges and needn't reach their ends.
All inputs are finite; a program needn't handle non-finite values.
Results may differ from the reference program's by a relative error of at most 0.02.
Values may be sent and summed in bfloat16 or wider, within the bound.
A program may use at most 64 MiB of HBM per device.

```python
import math
import jax
import jax.numpy as jnp
from jax import lax

B = 512
NB = 256
N_REP = 8
N_SHARD = 32


def make_root(key, low, high, spread):
    first, second = jax.random.split(key)
    diagonal = jnp.exp(jax.random.uniform(first, (NB, B), jnp.float32, math.log(low), math.log(high)))
    scatter = jnp.clip(jax.random.normal(second, (NB, B, B), jnp.float32), -4.0, 4.0) * (spread / math.sqrt(B))
    return (scatter + diagonal[:, :, None] * jnp.eye(B, dtype=jnp.float32)[None]).astype(jnp.bfloat16)


def draw_root_left(key, part):
    key = jax.random.fold_in(key, 11)
    return make_root(key, 0.3, 3.0, 0.4)


def draw_root_right(key, part):
    key = jax.random.fold_in(key, 23)
    return make_root(key, 0.3, 3.0, 0.4)


def block_scale(stream_key, shape, pieces, low, top_value):
    def one(axis_at, blocks):
        draws = jax.random.uniform(jax.random.fold_in(jax.random.fold_in(stream_key, 6), axis_at), (blocks,), jnp.float32, low / len(pieces), top_value / len(pieces))
        return jnp.repeat(jnp.exp(draws), shape[axis_at] // blocks).reshape((-1,) + (1,) * (len(shape) - axis_at - 1))

    factor_of = one(*pieces[0])
    for cut in pieces[1:]:
        factor_of = factor_of * one(*cut)
    return factor_of


def gaussian(rng, extent, width, limit, cuts=(), kind=jnp.bfloat16):
    level = block_scale(rng, extent, cuts, -0.22, 0.18) if cuts else 1.0
    result = jax.random.normal(rng, extent, jnp.float32) * width * level
    return jnp.minimum(jnp.maximum(result, -limit), limit).astype(kind)


def setup_inputs(seed: int = 0) -> dict:
    splits = jax.random.split(jax.random.key(seed), 7)
    grad = gaussian(splits[0], (N_REP, B, NB * B), 1.0, 6.0, ((0, 8), (1, 32)))
    owner_rep = jax.vmap(lambda own: jax.random.permutation(own, N_REP))(jax.random.split(splits[1], N_SHARD)).reshape((N_SHARD, N_REP)).astype(jnp.int32)
    stat_left = gaussian(splits[2], (NB, B, B), 0.5, 4.0, ((0, 256),), jnp.float32)
    stat_right = gaussian(splits[3], (NB, B, B), 0.5, 4.0, ((0, 256),), jnp.float32)
    root_left = draw_root_left(jax.random.fold_in(splits[6], 71), 0)
    root_right = draw_root_right(jax.random.fold_in(splits[6], 71), 0)
    return dict(grad=grad, owner_rep=owner_rep, stat_left=stat_left, stat_right=stat_right, root_left=root_left, root_right=root_right)


decay_rate = 0.9

def inverse_slots(owner_rep):
    count = owner_rep.shape[1]
    places = jnp.arange(count, dtype=jnp.int32)
    match = owner_rep[:, :, None] == places[None, None, :]
    return lax.optimization_barrier(jnp.sum(jnp.where(match, places[None, :, None], 0), axis=1)).astype(jnp.int32)

def reference(grad, owner_rep, stat_left, stat_right, root_left, root_right):
    total = grad[0].astype(jnp.float32)
    for replica in range(1, N_REP):
        total = total + grad[replica].astype(jnp.float32)
    blocks = total.reshape(B, NB, B)
    inverse = inverse_slots(owner_rep)
    source = (jnp.arange(N_SHARD, dtype=jnp.int32)[None, :] * N_REP + inverse.T).reshape(-1).astype(jnp.int32)
    highest = lax.Precision.HIGHEST

    def one_owner(owner):
        index = source[owner]
        block = lax.dynamic_index_in_dim(blocks, index, 1, keepdims=False)
        left_old = lax.dynamic_index_in_dim(stat_left, owner, 0, keepdims=False)
        right_old = lax.dynamic_index_in_dim(stat_right, owner, 0, keepdims=False)
        left_root = lax.dynamic_index_in_dim(root_left, owner, 0, keepdims=False)
        right_root = lax.dynamic_index_in_dim(root_right, owner, 0, keepdims=False)
        outer_left = jnp.dot(block, block.T, precision=highest, preferred_element_type=jnp.float32)
        outer_right = jnp.dot(block.T, block, precision=highest, preferred_element_type=jnp.float32)
        left_new = decay_rate * left_old + (1.0 - decay_rate) / B * outer_left
        right_new = decay_rate * right_old + (1.0 - decay_rate) / B * outer_right
        rounded = block.astype(jnp.bfloat16)
        half = jnp.dot(rounded, right_root, preferred_element_type=jnp.float32).astype(jnp.bfloat16)
        pre = jnp.dot(left_root, half, preferred_element_type=jnp.float32)
        scale = jnp.sqrt(jnp.sum(block * block) / (jnp.sum(pre * pre) + 1e-06))
        return (left_new, right_new, (-(scale * pre)).astype(jnp.bfloat16))
    new_left, new_right, owned = lax.map(one_owner, jnp.arange(NB, dtype=jnp.int32))
    target = (owner_rep * N_SHARD + jnp.arange(N_SHARD, dtype=jnp.int32)[:, None]).reshape(-1).astype(jnp.int32)
    placed = jnp.take(owned, target, axis=0)
    update = jnp.transpose(placed, (1, 0, 2)).reshape(B, NB * B)
    return (new_left, new_right, update)
```

```python
import jax
import jax.numpy as jnp
from jax import lax
from jax.experimental import pallas as pl
from jax.experimental.pallas import tpu as pltpu
from jax.sharding import PartitionSpec as P

MESH = pl.DeviceIdType.MESH
decay_rate = 0.9
ROWS = 16
SIDE = 512
LAG = 4
F32 = jnp.float32
BF16 = jnp.bfloat16


def rem(a, b):
    return lax.rem(a, jnp.int32(b))


def div(a, b):
    return lax.div(a, jnp.int32(b))


def exchange_kernel(
    inv_ref, grad_ref, rl_ref, rr_ref,
    all_ref, g_ref,
    grad_v, rl_v, rr_v, cs, cr, zs, zr, kp, ds, dr, half_v, pre_v, u_v, av,
    load_sem, root_sem, cs_sem, cr_sem, zs_sem, zr_sem, ds_sem, dr_sem,
    us_sem, ur_sem, fs_sem, fr_sem, hs_sem, hr_sem, keep_sem,
):
    rep = lax.axis_index("rep")
    s = lax.axis_index("shard")
    l, c = div(rep, 2), rem(rep, 2)
    x, h, y = div(s, 8), rem(div(s, 4), 2), rem(s, 4)
    z = h * 4 + l
    sgn = 2 * rem(l, 2) - 1
    rep_core = l * 2 + (1 - c)
    rep_pair = (l - sgn) * 2 + c

    load = pltpu.make_async_copy(grad_ref.at[0], grad_v, load_sem)
    load.start()
    load_l = pltpu.make_async_copy(rl_ref.at[0], rl_v, root_sem.at[0])
    load_r = pltpu.make_async_copy(rr_ref.at[0], rr_v, root_sem.at[1])
    load_l.start()
    load_r.start()

    def ring_z(offset):
        return rem(z + sgn * offset + 8, 8)

    def toward(m):
        return rem(x + div(m, 4), 4), rem(y + rem(m, 4), 4)

    def fro(m):
        return rem(x + 4 - div(m, 4), 4), rem(y + 4 - rem(m, 4), 4)

    def place(x2, y2, z2):
        return x2 * 8 + div(z2, 4) * 4 + y2

    def to(z2, x2, y2):
        return (rem(z2, 4) * 2 + c, place(x2, y2, z2))

    barrier = pltpu.get_barrier_semaphore()

    def greet(device):
        pl.semaphore_signal(barrier, inc=1, device_id=device, device_id_type=MESH)

    greet((rep_core, s))
    greet((rep_pair, s))
    for offset in (1, 2, 3, -2):
        greet(to(ring_z(offset), x, y))

    def greet_step(m, carry):
        x2, y2 = toward(m)
        for offset in (0, 1, 2, 3, -2):
            greet(to(ring_z(offset), x2, y2))
        return carry

    lax.fori_loop(1, 16, greet_step, 0)

    def block_of(x2, y2, z2, core):
        s2 = place(x2, y2, z2)
        slot = inv_ref[s2, rem(z2, 4) * 2 + core]
        column = (s2 * 8 + slot) * SIDE
        return grad_v[:, pl.ds(column, SIDE)]

    offsets = (0, 1, 2, 3, -1, -2, -3, -4)

    def remote(src, dst, send, recv, device):
        return pltpu.make_async_remote_copy(
            src_ref=src, dst_ref=dst, send_sem=send, recv_sem=recv,
            device_id=device, device_id_type=MESH,
        )

    def drain(ref, sem):
        pltpu.make_async_copy(ref, ref, sem).wait()

    load.wait()
    pl.semaphore_wait(barrier, 81)

    def core_step(m, carry):
        x2, y2 = toward(m)
        for e in range(8):
            cs[m, e] = block_of(x2, y2, ring_z(offsets[e]), 1 - c)
        remote(cs.at[m], cr.at[m], cs_sem, cr_sem.at[m], (rep_core, s)).start()
        return carry

    lax.fori_loop(0, 16, core_step, 0)

    def pair_step(m):
        x2, y2 = toward(m)
        drain(cr.at[m], cr_sem.at[m])
        for e in range(4, 8):
            zs[m, e - 4] = cr[m, e] + block_of(x2, y2, ring_z(offsets[e]), c)
        remote(zs.at[m], zr.at[m], zs_sem, zr_sem.at[m], (rep_pair, s)).start()
        for e in range(4):
            kp[m, e] = cr[m, e] + block_of(x2, y2, ring_z(offsets[e]), c)

    row = div(l, 2) * SIDE + s * ROWS

    def owner_step(m, first):
        x2, y2 = toward(m)
        drain(zr.at[m], zr_sem.at[m])
        target = dr.at[pl.ds(pl.multiple_of(row, ROWS), ROWS)]
        for i in range(4):
            ds[m, i] = zr[m, i] + kp[m, i]
            if first and i == 0:
                pltpu.make_async_copy(ds.at[m, i], target, dr_sem).start()
            else:
                remote(ds.at[m, i], target, ds_sem, dr_sem, to(ring_z(i), x2, y2)).start()

    def pair_only(m, carry):
        pair_step(m)
        return carry

    def pair_owner(m, carry):
        pair_step(m)
        owner_step(m - LAG + 1, False)
        return carry

    def owner_only(m, carry):
        owner_step(m, False)
        return carry

    lax.fori_loop(0, LAG, pair_only, 0)
    owner_step(0, True)
    lax.fori_loop(LAG, 16, pair_owner, 0)
    lax.fori_loop(16 - LAG + 1, 16, owner_only, 0)

    load_l.wait()
    load_r.wait()
    drain(dr, dr_sem)

    part = SIDE // 4

    def half_step(t, total):
        rows = pl.ds(pl.multiple_of(t * part, part), part)
        more = pl.ds(pl.multiple_of(SIDE + t * part, part), part)
        block = dr[rows, :].astype(F32) + dr[more, :].astype(F32)
        rounded = block.astype(BF16)
        g_ref[rows, :] = rounded
        half = jnp.dot(rounded, rr_v[...], preferred_element_type=F32)
        half_v[rows, :] = half.astype(BF16)
        return total + jnp.sum((block * block).reshape(part // 8, 8, SIDE), axis=0)

    zero = jnp.zeros((8, SIDE), F32)
    total_g = lax.fori_loop(0, 4, half_step, zero)

    def pre_step(t, total):
        rows = pl.ds(pl.multiple_of(t * part, part), part)
        pre = jnp.dot(rl_v[rows, :], half_v[...], preferred_element_type=F32)
        pre_v[rows, :] = pre
        return total + jnp.sum((pre * pre).reshape(part // 8, 8, SIDE), axis=0)

    total_p = lax.fori_loop(0, 4, pre_step, zero)
    scale = jnp.sqrt(
        jnp.sum(total_g, keepdims=True) / (jnp.sum(total_p, keepdims=True) + 1e-06)
    )

    def scale_step(t, carry):
        rows = pl.ds(pl.multiple_of(t * part, part), part)
        u_v[rows, :] = (-(scale * pre_v[rows, :])).astype(BF16)
        return carry

    lax.fori_loop(0, 4, scale_step, 0)

    def spread_step(m, first):
        x2, y2 = toward(m)
        for i in range(4):
            z2 = ring_z(-i if i % 2 == 0 else i)
            device = to(z2, x2, y2)
            source = u_v.at[pl.ds(pl.multiple_of(device[1] * ROWS, ROWS), ROWS)]
            if first and i == 0:
                pltpu.make_async_copy(source, av.at[s, l], ur_sem.at[m]).start()
            else:
                remote(source, av.at[s, l], us_sem, ur_sem.at[m], device).start()

    def spread_loop(m, carry):
        spread_step(m, False)
        return carry

    spread_step(0, True)
    lax.fori_loop(1, 16, spread_loop, 0)

    def forward_pair(m):
        x1, y1 = fro(m)
        drain(av.at[0], ur_sem.at[m])
        for i in range(4):
            d = ring_z(i)
            slot = av.at[place(x1, y1, d), rem(d, 4)]
            remote(slot, slot, fs_sem, fr_sem.at[m], (rep_pair, s)).start()

    def forward_core(m):
        x1, y1 = fro(m)
        drain(av.at[0], fr_sem.at[m])
        for i in range(2):
            s1 = x1 * 8 + i * 4 + y1
            remote(av.at[s1], all_ref.at[s1, c], hs_sem, hr_sem, (rep_core, s)).start()
            pltpu.make_async_copy(av.at[s1], all_ref.at[s1, c], keep_sem).start()

    def forward_first(m, carry):
        forward_pair(m)
        return carry

    def forward_both(m, carry):
        forward_pair(m)
        forward_core(m - LAG)
        return carry

    def forward_last(m, carry):
        forward_core(m)
        return carry

    lax.fori_loop(0, LAG, forward_first, 0)
    lax.fori_loop(LAG, 16, forward_both, 0)
    lax.fori_loop(16 - LAG, 16, forward_last, 0)

    drain(cs, cs_sem)
    drain(zs, zs_sem)
    drain(dr.at[pl.ds(0, 63 * ROWS)], ds_sem)
    drain(dr.at[pl.ds(0, 63 * ROWS)], us_sem)
    drain(zs, fs_sem)
    drain(av, keep_sem)
    drain(av, hs_sem)
    drain(av, hr_sem)


def exchange(inverse, grad, root_left, root_right):
    any_space = pl.BlockSpec(memory_space=pl.ANY)
    dma = pltpu.SemaphoreType.DMA
    blk = (ROWS, SIDE)
    return pl.pallas_call(
        exchange_kernel,
        out_shape=(
            jax.ShapeDtypeStruct((32, 2, 4) + blk, BF16),
            jax.ShapeDtypeStruct((SIDE, SIDE), BF16),
        ),
        in_specs=[pl.BlockSpec(memory_space=pltpu.SMEM), any_space, any_space, any_space],
        out_specs=(any_space, pl.BlockSpec(memory_space=pltpu.VMEM)),
        scratch_shapes=[
            pltpu.VMEM((ROWS, 256 * SIDE), BF16),
            pltpu.VMEM((SIDE, SIDE), BF16),
            pltpu.VMEM((SIDE, SIDE), BF16),
            pltpu.VMEM((16, 8) + blk, BF16),
            pltpu.VMEM((16, 8) + blk, BF16),
            pltpu.VMEM((16, 4) + blk, BF16),
            pltpu.VMEM((16, 4) + blk, BF16),
            pltpu.VMEM((16, 4) + blk, BF16),
            pltpu.VMEM((16, 4) + blk, BF16),
            pltpu.VMEM((2 * SIDE, SIDE), BF16),
            pltpu.VMEM((SIDE, SIDE), BF16),
            pltpu.VMEM((SIDE, SIDE), F32),
            pltpu.VMEM((SIDE, SIDE), BF16),
            pltpu.VMEM((32, 4) + blk, BF16),
            dma, dma((2,)), dma, dma((16,)), dma, dma((16,)), dma, dma,
            dma, dma((16,)), dma, dma((16,)), dma, dma, dma,
        ],
        compiler_params=pltpu.CompilerParams(
            collective_id=0, has_side_effects=True, vmem_limit_bytes=56 * 1024 * 1024
        ),
    )(inverse, grad, root_left, root_right)


STEPS = 8


def finish_kernel(own_ref, all_ref, g_ref, left_ref, right_ref, new_left_ref, new_right_ref, update_ref):
    t = pl.program_id(0)
    part = SIDE // STEPS
    factor = (1.0 - decay_rate) / SIDE
    whole = g_ref[...]
    rows = g_ref[pl.ds(pl.multiple_of(t * part, part), part), :]
    outer = lax.dot_general(rows, whole, (((1,), (1,)), ((), ())), preferred_element_type=F32)
    new_left_ref[0] = decay_rate * left_ref[0] + factor * outer

    for step in range(0, STEPS, 2):
        @pl.when(div(t, 2) == step // 2)
        def _():
            cols = g_ref[:, step * part:(step + 2) * part]
            inner = lax.dot_general(cols, whole, (((0,), (0,)), ((), ())), preferred_element_type=F32)

            @pl.when(rem(t, 2) == 0)
            def _():
                new_right_ref[0] = decay_rate * right_ref[0] + factor * inner[:part]

            @pl.when(rem(t, 2) == 1)
            def _():
                new_right_ref[0] = decay_rate * right_ref[0] + factor * inner[part:]

    count = 32 // STEPS

    def column(q, carry):
        for k in range(8):
            r = own_ref[t * count + q, k]
            index = q * 8 + rem(r, 2) * 4 + div(r, 2)
            at = pl.multiple_of((q * 8 + k) * SIDE, SIDE)
            update_ref[:, pl.ds(at, SIDE)] = all_ref[index]
        return carry

    lax.fori_loop(0, count, column, 0)


def finish(owner_rep, collected, block, stat_left, stat_right):
    part = SIDE // STEPS
    stat = pl.BlockSpec((1, part, SIDE), lambda t, own: (0, t, 0))
    return pl.pallas_call(
        finish_kernel,
        out_shape=(
            jax.ShapeDtypeStruct((1, SIDE, SIDE), F32),
            jax.ShapeDtypeStruct((1, SIDE, SIDE), F32),
            jax.ShapeDtypeStruct((ROWS, 256 * SIDE), BF16),
        ),
        grid_spec=pltpu.PrefetchScalarGridSpec(
            num_scalar_prefetch=1,
            grid=(STEPS,),
            in_specs=[
                pl.BlockSpec((256 // STEPS, ROWS, SIDE), lambda t, own: (t, 0, 0)),
                pl.BlockSpec((SIDE, SIDE), lambda t, own: (0, 0)),
                stat,
                stat,
            ],
            out_specs=(
                stat,
                stat,
                pl.BlockSpec((ROWS, 256 * SIDE // STEPS), lambda t, own: (0, t)),
            ),
        ),
        compiler_params=pltpu.CompilerParams(vmem_limit_bytes=32 * 1024 * 1024),
    )(owner_rep, collected, block, stat_left, stat_right)


def inverse_slots(owner_rep):
    places = jnp.arange(8, dtype=jnp.int32)
    match = owner_rep[:, :, None] == places[None, None, :]
    return jnp.sum(jnp.where(match, places[None, :, None], 0), axis=1).astype(jnp.int32)


def body(grad, owner_rep, stat_left, stat_right, root_left, root_right):
    inverse = inverse_slots(owner_rep)
    collected, block = exchange(inverse, grad, root_left, root_right)
    collected = collected.reshape(256, ROWS, SIDE)
    return finish(owner_rep, collected, block, stat_left, stat_right)


def solution(mesh):
    owned = P(("rep", "shard"), None, None)
    return jax.shard_map(
        body,
        mesh=mesh,
        in_specs=(P("rep", "shard", None), P(), owned, owned, owned, owned),
        out_specs=(owned, owned, P("shard", None)),
        check_vma=False,
    )
```

```python
import jax
import jax.numpy as jnp
from jax import lax
from jax.experimental import pallas as pl
from jax.experimental.pallas import tpu as pltpu
from jax.sharding import PartitionSpec as P

MESH = pl.DeviceIdType.MESH
decay_rate = 0.9
ROWS = 16
SIDE = 512
AHEAD = 2
LAG = 4
WINDOW = 4
TRAIL = 3
FAR = (3, 2, 1, 0)
VMEM_MIB = 40
F32 = jnp.float32
BF16 = jnp.bfloat16


def rem(a, b):
    return lax.rem(a, jnp.int32(b))


def div(a, b):
    return lax.div(a, jnp.int32(b))


def exchange_kernel(
    own_ref, grad_ref, rl_ref, rr_ref, left_ref, right_ref,
    new_left_ref, new_right_ref, update_ref,
    own_v, own_s, inv_v, inv_s, grad_v, rl_v, rr_v, left_v, right_v,
    cs, cr, zs, zr, kp, ds, dr, g_v, half_v, pre_v, u_v, av,
    own_sem, load_sem, root_sem, stat_sem, cs_sem, cr_sem, zs_sem, zr_sem, ds_sem, dr_sem,
    us_sem, ur_sem, fs_sem, fr_sem, hs_sem, hr_sem, plane_sem, block_sem,
):
    rep = lax.axis_index("rep")
    s = lax.axis_index("shard")
    l, c = div(rep, 2), rem(rep, 2)
    x, h, y = div(s, 8), rem(div(s, 4), 2), rem(s, 4)
    z = h * 4 + l
    sgn = 2 * rem(l, 2) - 1
    rep_core = l * 2 + (1 - c)
    rep_pair = (l - sgn) * 2 + c

    own_load = pltpu.make_async_copy(own_ref, own_v, own_sem.at[0])
    own_load.start()
    slot_load = pltpu.make_async_copy(own_ref, own_s, own_sem.at[1])
    slot_load.start()
    load = pltpu.make_async_copy(grad_ref.at[0], grad_v, load_sem)
    load.start()
    later = [
        pltpu.make_async_copy(rl_ref.at[0], rl_v, root_sem.at[0]),
        pltpu.make_async_copy(rr_ref.at[0], rr_v, root_sem.at[1]),
        pltpu.make_async_copy(left_ref.at[0], left_v, stat_sem.at[0]),
        pltpu.make_async_copy(right_ref.at[0], right_v, stat_sem.at[1]),
    ]

    def ring_z(offset):
        return rem(z + sgn * offset + 8, 8)

    def toward(m):
        return rem(x + div(m, 4), 4), rem(y + rem(m, 4), 4)

    def fro(m):
        return rem(x + 4 - div(m, 4), 4), rem(y + 4 - rem(m, 4), 4)

    def place(x2, y2, z2):
        return x2 * 8 + div(z2, 4) * 4 + y2

    def to(z2, x2, y2):
        return (rem(z2, 4) * 2 + c, place(x2, y2, z2))

    barrier = pltpu.get_barrier_semaphore()

    def greet(sem, device):
        pl.semaphore_signal(sem, inc=1, device_id=device, device_id_type=MESH)

    greet(barrier, (rep_core, s))
    for offset in (-1, 1, 2, 3, -2):
        greet(barrier, to(ring_z(offset), x, y))
    for step in (1, 2, 3):
        greet(barrier, to(z, rem(x + step, 4), y))
        greet(barrier, to(z, x, rem(y + step, 4)))

    own_load.wait()
    owners = own_v[...]
    lines = []
    for r in range(8):
        line = jnp.zeros((1, 32), jnp.int32)
        for k in range(1, 8):
            line = jnp.where(owners[k:k + 1] == r, k, line)
        lines.append(line)
    inv_v[...] = jnp.concatenate(lines, axis=0)
    inv_load = pltpu.make_async_copy(inv_v, inv_s, own_sem.at[2])
    inv_load.start()

    def block_of(x2, y2, z2, core):
        s2 = place(x2, y2, z2)
        slot = inv_s[rem(z2, 4) * 2 + core, s2]
        column = (s2 * 8 + slot) * SIDE
        return grad_v[:, pl.ds(column, SIDE)]

    offsets = (0, 1, 2, 3, -1, -2, -3, -4)

    def remote(src, dst, send, recv, device):
        return pltpu.make_async_remote_copy(
            src_ref=src, dst_ref=dst, send_sem=send, recv_sem=recv,
            device_id=device, device_id_type=MESH,
        )

    def drain(ref, sem):
        pltpu.make_async_copy(ref, ref, sem).wait()

    inv_load.wait()
    load.wait()
    pl.semaphore_wait(barrier, 12)
    for step in (1, 2, 3):
        greet(plane_sem, to(z, x, rem(y + step, 4)))

    def core_step(m):
        x2, y2 = toward(m)
        for e in range(8):
            cs[m, e] = block_of(x2, y2, ring_z(offsets[e]), 1 - c)
        remote(cs.at[m], cr.at[m], cs_sem, cr_sem.at[m], (rep_core, s)).start()

    def pair_step(m):
        x2, y2 = toward(m)
        drain(cr.at[m], cr_sem.at[m])
        for i in FAR:
            zs[m, i] = cr[m, i + 4] + block_of(x2, y2, ring_z(offsets[i + 4]), c)
            remote(zs.at[m, i], zr.at[m, i], zs_sem, zr_sem.at[m, i], (rep_pair, s)).start()
        for e in range(4):
            kp[m, e] = cr[m, e] + block_of(x2, y2, ring_z(offsets[e]), c)

    row = div(l, 2) * SIDE + s * ROWS

    def owner_step(m):
        x2, y2 = toward(m)
        target = dr.at[pl.ds(pl.multiple_of(row, ROWS), ROWS)]
        for i in FAR:
            drain(zr.at[m, i], zr_sem.at[m, i])
            ds[m, i] = zr[m, i] + kp[m, i]

            def send():
                remote(ds.at[m, i], target, ds_sem, dr_sem, to(ring_z(i), x2, y2)).start()

            if i == 0:
                @pl.when(m == 0)
                def _():
                    pltpu.make_async_copy(ds.at[m, i], target, dr_sem).start()

                pl.when(m > 0)(send)
            else:
                send()

    def collect_step(t, carry):
        @pl.when(t < 16)
        def _():
            core_step(t)

        @pl.when((t >= AHEAD) & (t < 16 + AHEAD))
        def _():
            pair_step(t - AHEAD)

        @pl.when(t == AHEAD)
        def _():
            pl.semaphore_wait(plane_sem, 3)
            for offset in (1, 2, 3, -2):
                greet(block_sem, to(ring_z(offset), x, y))

        @pl.when(t == AHEAD + LAG)
        def _():
            pl.semaphore_wait(block_sem, 4)

        @pl.when(t >= AHEAD + LAG)
        def _():
            owner_step(t - AHEAD - LAG)
        return carry

    lax.fori_loop(0, 1, collect_step, 0)
    for copy in later:
        copy.start()
    lax.fori_loop(1, 16 + AHEAD + LAG, collect_step, 0)

    for copy in later:
        copy.wait()
    slot_load.wait()
    drain(dr, dr_sem)

    part = SIDE // 4

    def half_step(t, total):
        rows = pl.ds(pl.multiple_of(t * part, part), part)
        more = pl.ds(pl.multiple_of(SIDE + t * part, part), part)
        block = dr[rows, :].astype(F32) + dr[more, :].astype(F32)
        rounded = block.astype(BF16)
        g_v[rows, :] = rounded
        half = jnp.dot(rounded, rr_v[...], preferred_element_type=F32)
        half_v[rows, :] = half.astype(BF16)
        return total + jnp.sum((block * block).reshape(part // 8, 8, SIDE), axis=0)

    zero = jnp.zeros((8, SIDE), F32)
    total_g = lax.fori_loop(0, 4, half_step, zero)

    def pre_step(t, total):
        rows = pl.ds(pl.multiple_of(t * part, part), part)
        pre = jnp.dot(rl_v[rows, :], half_v[...], preferred_element_type=F32)
        pre_v[rows, :] = pre
        return total + jnp.sum((pre * pre).reshape(part // 8, 8, SIDE), axis=0)

    total_p = lax.fori_loop(0, 4, pre_step, zero)
    scale = jnp.sqrt(
        jnp.sum(total_g, keepdims=True) / (jnp.sum(total_p, keepdims=True) + 1e-06)
    )

    def scale_step(t, carry):
        rows = pl.ds(pl.multiple_of(t * part, part), part)
        u_v[rows, :] = (-(scale * pre_v[rows, :])).astype(BF16)
        return carry

    lax.fori_loop(0, 4, scale_step, 0)

    def spread(m):
        x2, y2 = toward(m)
        for i in range(4):
            z2 = ring_z(-i if i % 2 == 0 else i)
            device = to(z2, x2, y2)
            source = u_v.at[pl.ds(pl.multiple_of(device[1] * ROWS, ROWS), ROWS)]

            def send():
                remote(source, av.at[m, h, c, l], us_sem, ur_sem.at[m, i], device).start()

            if i == 0:
                @pl.when(m == 0)
                def _():
                    pltpu.make_async_copy(source, av.at[m, h, c, l], ur_sem.at[m, i]).start()

                pl.when(m > 0)(send)
            else:
                send()

    def forward_pair(m):
        for i in range(4):
            d = ring_z(i)
            slot = av.at[m, div(d, 4), c, rem(d, 4)]
            drain(slot, ur_sem.at[m, i])
            remote(slot, slot, fs_sem, fr_sem.at[m], (rep_pair, s)).start()

    def forward_core(m):
        drain(av.at[m, 0, c], fr_sem.at[m])
        for i in range(2):
            slot = av.at[m, i, c]
            remote(slot, slot, hs_sem, hr_sem.at[m], (rep_core, s)).start()

    def arrange(m):
        x1, y1 = fro(m)
        drain(av.at[m, 0], hr_sem.at[m])
        for i in range(2):
            s1 = x1 * 8 + i * 4 + y1
            slots = [own_s[k, s1] for k in range(8)]
            for q in range(4):
                lanes = pl.ds(q * 128, 128)
                pieces = [av[m, i, r % 2, r // 2, :, lanes] for r in range(8)]
                for k in range(8):
                    piece = pieces[0]
                    for r in range(1, 8):
                        piece = jnp.where(slots[k] == r, pieces[r], piece)
                    at = pl.multiple_of((s1 * 8 + k) * SIDE + q * 128, 128)
                    update_ref[:, pl.ds(at, 128)] = piece

    factor = (1.0 - decay_rate) / SIDE

    def stats(t):
        rows = pl.ds(pl.multiple_of(t * part, part), part)
        outer = lax.dot_general(
            g_v[rows, :], g_v[...], (((1,), (1,)), ((), ())), preferred_element_type=F32
        )
        new_left_ref[0, rows, :] = decay_rate * left_v[rows, :] + factor * outer
        inner = lax.dot_general(
            g_v[:, rows], g_v[...], (((0,), (0,)), ((), ())), preferred_element_type=F32
        )
        new_right_ref[0, rows, :] = decay_rate * right_v[rows, :] + factor * inner

    def spread_step(t, carry):
        @pl.when(t < 16)
        def _():
            spread(t)

        @pl.when((t >= WINDOW) & (t < 16 + WINDOW))
        def _():
            forward_pair(t - WINDOW)

        @pl.when((t >= WINDOW + TRAIL) & (t < 16 + WINDOW + TRAIL))
        def _():
            forward_core(t - WINDOW - TRAIL)

        @pl.when((t >= WINDOW + 2) & (t < WINDOW + 6))
        def _():
            stats(t - WINDOW - 2)

        @pl.when(t >= WINDOW + TRAIL + 1)
        def _():
            arrange(t - WINDOW - TRAIL - 1)
        return carry

    lax.fori_loop(0, 17 + WINDOW + TRAIL, spread_step, 0)

    drain(cs, cs_sem)
    drain(zs, zs_sem)
    drain(dr.at[pl.ds(0, 63 * ROWS)], ds_sem)
    drain(dr.at[pl.ds(0, 63 * ROWS)], us_sem)
    drain(zs, fs_sem)
    drain(zs, hs_sem)
    drain(zs, hs_sem)


def exchange(owner_rep, grad, root_left, root_right, stat_left, stat_right):
    held = [
        pltpu.with_memory_space_constraint(v, pltpu.HBM)
        for v in (owner_rep.T, grad, root_left, root_right, stat_left, stat_right)
    ]
    any_space = pl.BlockSpec(memory_space=pl.ANY)
    vmem = pl.BlockSpec(memory_space=pltpu.VMEM)
    dma = pltpu.SemaphoreType.DMA
    blk = (ROWS, SIDE)
    square = (SIDE, SIDE)
    return pl.pallas_call(
        exchange_kernel,
        out_shape=(
            jax.ShapeDtypeStruct((1,) + square, F32),
            jax.ShapeDtypeStruct((1,) + square, F32),
            jax.ShapeDtypeStruct((ROWS, 256 * SIDE), BF16),
        ),
        in_specs=[any_space] * 6,
        out_specs=(vmem, vmem, vmem),
        scratch_shapes=[
            pltpu.VMEM((8, 32), jnp.int32),
            pltpu.SMEM((8, 32), jnp.int32),
            pltpu.VMEM((8, 32), jnp.int32),
            pltpu.SMEM((8, 32), jnp.int32),
            pltpu.VMEM((ROWS, 256 * SIDE), BF16),
            pltpu.VMEM(square, BF16),
            pltpu.VMEM(square, BF16),
            pltpu.VMEM(square, F32),
            pltpu.VMEM(square, F32),
            pltpu.VMEM((16, 8) + blk, BF16),
            pltpu.VMEM((16, 8) + blk, BF16),
            pltpu.VMEM((16, 4) + blk, BF16),
            pltpu.VMEM((16, 4) + blk, BF16),
            pltpu.VMEM((16, 4) + blk, BF16),
            pltpu.VMEM((16, 4) + blk, BF16),
            pltpu.VMEM((2 * SIDE, SIDE), BF16),
            pltpu.VMEM(square, BF16),
            pltpu.VMEM(square, BF16),
            pltpu.VMEM(square, F32),
            pltpu.VMEM(square, BF16),
            pltpu.VMEM((16, 2, 2, 4) + blk, BF16),
            dma((3,)), dma, dma((2,)), dma((2,)), dma, dma((16,)), dma, dma((16, 4)), dma, dma,
            dma, dma((16, 4)), dma, dma((16,)), dma, dma((16,)),
            pltpu.SemaphoreType.REGULAR, pltpu.SemaphoreType.REGULAR,
        ],
        compiler_params=pltpu.CompilerParams(
            collective_id=0, has_side_effects=True, vmem_limit_bytes=VMEM_MIB * 1024 * 1024
        ),
    )(*held)


def body(grad, owner_rep, stat_left, stat_right, root_left, root_right):
    return exchange(owner_rep, grad, root_left, root_right, stat_left, stat_right)


def solution(mesh):
    owned = P(("rep", "shard"), None, None)
    return jax.shard_map(
        body,
        mesh=mesh,
        in_specs=(P("rep", "shard", None), P(), owned, owned, owned, owned),
        out_specs=(owned, owned, P("shard", None)),
        check_vma=False,
    )
```

```python
import jax
import jax.numpy as jnp
from jax import lax
from jax.experimental import pallas as pl
from jax.experimental.pallas import tpu as pltpu
from jax.sharding import PartitionSpec as P

MESH = pl.DeviceIdType.MESH
decay_rate = 0.9
ROWS = 16
SIDE = 512
GATE = 16
LAG = 4
WINDOW = 4
TRAIL = 3
FAR = (3, 2, 1, 0)
VMEM_MIB = 40
F32 = jnp.float32
BF16 = jnp.bfloat16


def rem(a, b):
    return lax.rem(a, jnp.int32(b))


def div(a, b):
    return lax.div(a, jnp.int32(b))


def exchange_kernel(
    own_ref, grad_ref, rl_ref, rr_ref, left_ref, right_ref,
    new_left_ref, new_right_ref, update_ref,
    own_v, own_s, inv_v, inv_s, grad_v, rl_v, rr_v, left_v, right_v,
    cs, cr, zs, zr, kp, ds, dr, g_v, half_v, pre_v, u_v, av,
    own_sem, load_sem, root_sem, stat_sem, cs_sem, cr_sem, zs_sem, zr_sem, ds_sem, dr_sem,
    us_sem, ur_sem, fs_sem, fr_sem, hs_sem, hr_sem, plane_sem, block_sem, gate_sem,
):
    rep = lax.axis_index("rep")
    s = lax.axis_index("shard")
    l, c = div(rep, 2), rem(rep, 2)
    x, h, y = div(s, 8), rem(div(s, 4), 2), rem(s, 4)
    z = h * 4 + l
    sgn = 2 * rem(l, 2) - 1
    rep_core = l * 2 + (1 - c)
    rep_pair = (l - sgn) * 2 + c

    own_load = pltpu.make_async_copy(own_ref, own_v, own_sem.at[0])
    own_load.start()
    slot_load = pltpu.make_async_copy(own_ref, own_s, own_sem.at[1])
    slot_load.start()
    load = pltpu.make_async_copy(grad_ref.at[0], grad_v, load_sem)
    load.start()
    later = [
        pltpu.make_async_copy(rl_ref.at[0], rl_v, root_sem.at[0]),
        pltpu.make_async_copy(rr_ref.at[0], rr_v, root_sem.at[1]),
        pltpu.make_async_copy(left_ref.at[0], left_v, stat_sem.at[0]),
        pltpu.make_async_copy(right_ref.at[0], right_v, stat_sem.at[1]),
    ]

    def ring_z(offset):
        return rem(z + sgn * offset + 8, 8)

    def toward(m):
        return rem(x + div(m, 4), 4), rem(y + rem(m, 4), 4)

    def fro(m):
        return rem(x + 4 - div(m, 4), 4), rem(y + 4 - rem(m, 4), 4)

    def place(x2, y2, z2):
        return x2 * 8 + div(z2, 4) * 4 + y2

    def to(z2, x2, y2):
        return (rem(z2, 4) * 2 + c, place(x2, y2, z2))

    barrier = pltpu.get_barrier_semaphore()

    def greet(sem, device):
        pl.semaphore_signal(sem, inc=1, device_id=device, device_id_type=MESH)

    greet(barrier, (rep_core, s))
    for offset in (-1, 1, 2, 3, -2):
        greet(barrier, to(ring_z(offset), x, y))
    for step in (1, 2, 3):
        greet(barrier, to(z, rem(x + step, 4), y))
        greet(barrier, to(z, x, rem(y + step, 4)))

    own_load.wait()
    owners = own_v[...]
    lines = []
    for r in range(8):
        line = jnp.zeros((1, 32), jnp.int32)
        for k in range(1, 8):
            line = jnp.where(owners[k:k + 1] == r, k, line)
        lines.append(line)
    inv_v[...] = jnp.concatenate(lines, axis=0)
    inv_load = pltpu.make_async_copy(inv_v, inv_s, own_sem.at[2])
    inv_load.start()

    def block_of(x2, y2, z2, core):
        s2 = place(x2, y2, z2)
        slot = inv_s[rem(z2, 4) * 2 + core, s2]
        column = (s2 * 8 + slot) * SIDE
        return grad_v[:, pl.ds(column, SIDE)]

    offsets = (0, 1, 2, 3, -1, -2, -3, -4)

    def remote(src, dst, send, recv, device):
        return pltpu.make_async_remote_copy(
            src_ref=src, dst_ref=dst, send_sem=send, recv_sem=recv,
            device_id=device, device_id_type=MESH,
        )

    def drain(ref, sem):
        pltpu.make_async_copy(ref, ref, sem).wait()

    inv_load.wait()
    load.wait()
    pl.semaphore_wait(barrier, 12)
    for step in (1, 2, 3):
        greet(plane_sem, to(z, x, rem(y + step, 4)))

    def core_step(m):
        x2, y2 = toward(m)
        for e in range(8):
            cs[m, e] = block_of(x2, y2, ring_z(offsets[e]), 1 - c)
        remote(cs.at[m], cr.at[m], cs_sem, cr_sem.at[m], (rep_core, s)).start()

    def pair_step(m):
        x2, y2 = toward(m)
        drain(cr.at[m], cr_sem.at[m])
        for i in FAR:
            zs[m, i] = cr[m, i + 4] + block_of(x2, y2, ring_z(offsets[i + 4]), c)
            remote(zs.at[m, i], zr.at[m, i], zs_sem, zr_sem.at[m, i], (rep_pair, s)).start()
        for e in range(4):
            kp[m, e] = cr[m, e] + block_of(x2, y2, ring_z(offsets[e]), c)

    row = div(l, 2) * SIDE + s * ROWS

    def owner_step(m):
        x2, y2 = toward(m)
        target = dr.at[pl.ds(pl.multiple_of(row, ROWS), ROWS)]
        for i in FAR:
            drain(zr.at[m, i], zr_sem.at[m, i])
            ds[m, i] = zr[m, i] + kp[m, i]

            def send():
                remote(ds.at[m, i], target, ds_sem, dr_sem, to(ring_z(i), x2, y2)).start()

            if i == 0:
                @pl.when(m == 0)
                def _():
                    pltpu.make_async_copy(ds.at[m, i], target, dr_sem).start()

                pl.when(m > 0)(send)
            else:
                send()

    def feed(m, carry):
        core_step(m)
        return carry

    def collect_step(t, carry):
        @pl.when(t < 16)
        def _():
            pair_step(t)

        @pl.when(t == 0)
        def _():
            pl.semaphore_wait(plane_sem, 3)
            for offset in (1, 2, 3, -2):
                greet(block_sem, to(ring_z(offset), x, y))

        @pl.when(t == LAG)
        def _():
            pl.semaphore_wait(block_sem, 4)

        @pl.when(t >= LAG)
        def _():
            owner_step(t - LAG)

        @pl.when((t >= LAG) & (c == 0))
        def _():
            core_step(t - LAG)

        @pl.when((t == GATE) & (c == 0))
        def _():
            greet(gate_sem, (rep_core, s))
        return carry

    lax.fori_loop(0, 16 * c, feed, 0)
    for copy in later:
        copy.start()

    @pl.when(c == 1)
    def _():
        pl.semaphore_wait(gate_sem, 1)

    lax.fori_loop(0, 16 + LAG, collect_step, 0)

    for copy in later:
        copy.wait()
    slot_load.wait()
    drain(dr, dr_sem)

    part = SIDE // 4

    def half_step(t, total):
        rows = pl.ds(pl.multiple_of(t * part, part), part)
        more = pl.ds(pl.multiple_of(SIDE + t * part, part), part)
        block = dr[rows, :].astype(F32) + dr[more, :].astype(F32)
        rounded = block.astype(BF16)
        g_v[rows, :] = rounded
        half = jnp.dot(rounded, rr_v[...], preferred_element_type=F32)
        half_v[rows, :] = half.astype(BF16)
        return total + jnp.sum((block * block).reshape(part // 8, 8, SIDE), axis=0)

    zero = jnp.zeros((8, SIDE), F32)
    total_g = lax.fori_loop(0, 4, half_step, zero)

    def pre_step(t, total):
        rows = pl.ds(pl.multiple_of(t * part, part), part)
        pre = jnp.dot(rl_v[rows, :], half_v[...], preferred_element_type=F32)
        pre_v[rows, :] = pre
        return total + jnp.sum((pre * pre).reshape(part // 8, 8, SIDE), axis=0)

    total_p = lax.fori_loop(0, 4, pre_step, zero)
    scale = jnp.sqrt(
        jnp.sum(total_g, keepdims=True) / (jnp.sum(total_p, keepdims=True) + 1e-06)
    )

    def scale_step(t, carry):
        rows = pl.ds(pl.multiple_of(t * part, part), part)
        u_v[rows, :] = (-(scale * pre_v[rows, :])).astype(BF16)
        return carry

    lax.fori_loop(0, 4, scale_step, 0)

    def spread(m):
        x2, y2 = toward(m)
        for i in range(4):
            z2 = ring_z(-i if i % 2 == 0 else i)
            device = to(z2, x2, y2)
            source = u_v.at[pl.ds(pl.multiple_of(device[1] * ROWS, ROWS), ROWS)]

            def send():
                remote(source, av.at[m, h, c, l], us_sem, ur_sem.at[m, i], device).start()

            if i == 0:
                @pl.when(m == 0)
                def _():
                    pltpu.make_async_copy(source, av.at[m, h, c, l], ur_sem.at[m, i]).start()

                pl.when(m > 0)(send)
            else:
                send()

    def forward_pair(m):
        for i in range(4):
            d = ring_z(i)
            slot = av.at[m, div(d, 4), c, rem(d, 4)]
            drain(slot, ur_sem.at[m, i])
            remote(slot, slot, fs_sem, fr_sem.at[m], (rep_pair, s)).start()

    def forward_core(m):
        drain(av.at[m, 0, c], fr_sem.at[m])
        for i in range(2):
            slot = av.at[m, i, c]
            remote(slot, slot, hs_sem, hr_sem.at[m], (rep_core, s)).start()

    def arrange(m):
        x1, y1 = fro(m)
        drain(av.at[m, 0], hr_sem.at[m])
        for i in range(2):
            s1 = x1 * 8 + i * 4 + y1
            slots = [own_s[k, s1] for k in range(8)]
            for q in range(4):
                lanes = pl.ds(q * 128, 128)
                pieces = [av[m, i, r % 2, r // 2, :, lanes] for r in range(8)]
                for k in range(8):
                    piece = pieces[0]
                    for r in range(1, 8):
                        piece = jnp.where(slots[k] == r, pieces[r], piece)
                    at = pl.multiple_of((s1 * 8 + k) * SIDE + q * 128, 128)
                    update_ref[:, pl.ds(at, 128)] = piece

    factor = (1.0 - decay_rate) / SIDE

    def stats(t):
        rows = pl.ds(pl.multiple_of(t * part, part), part)
        outer = lax.dot_general(
            g_v[rows, :], g_v[...], (((1,), (1,)), ((), ())), preferred_element_type=F32
        )
        new_left_ref[0, rows, :] = decay_rate * left_v[rows, :] + factor * outer
        inner = lax.dot_general(
            g_v[:, rows], g_v[...], (((0,), (0,)), ((), ())), preferred_element_type=F32
        )
        new_right_ref[0, rows, :] = decay_rate * right_v[rows, :] + factor * inner

    def spread_step(t, carry):
        @pl.when(t < 16)
        def _():
            spread(t)

        @pl.when((t >= WINDOW) & (t < 16 + WINDOW))
        def _():
            forward_pair(t - WINDOW)

        @pl.when((t >= WINDOW + TRAIL) & (t < 16 + WINDOW + TRAIL))
        def _():
            forward_core(t - WINDOW - TRAIL)

        @pl.when((t >= WINDOW + 2) & (t < WINDOW + 6))
        def _():
            stats(t - WINDOW - 2)

        @pl.when((t >= WINDOW + TRAIL + 1) & (c == 1))
        def _():
            arrange(t - WINDOW - TRAIL - 1)
        return carry

    def arrange_step(m, carry):
        arrange(m)
        return carry

    lax.fori_loop(0, 17 + WINDOW + TRAIL, spread_step, 0)
    lax.fori_loop(0, 16 * (1 - c), arrange_step, 0)

    drain(cs, cs_sem)
    drain(zs, zs_sem)
    drain(dr.at[pl.ds(0, 63 * ROWS)], ds_sem)
    drain(dr.at[pl.ds(0, 63 * ROWS)], us_sem)
    drain(zs, fs_sem)
    drain(zs, hs_sem)
    drain(zs, hs_sem)


def exchange(owner_rep, grad, root_left, root_right, stat_left, stat_right):
    held = [
        pltpu.with_memory_space_constraint(v, pltpu.HBM)
        for v in (owner_rep.T, grad, root_left, root_right, stat_left, stat_right)
    ]
    any_space = pl.BlockSpec(memory_space=pl.ANY)
    vmem = pl.BlockSpec(memory_space=pltpu.VMEM)
    dma = pltpu.SemaphoreType.DMA
    blk = (ROWS, SIDE)
    square = (SIDE, SIDE)
    return pl.pallas_call(
        exchange_kernel,
        out_shape=(
            jax.ShapeDtypeStruct((1,) + square, F32),
            jax.ShapeDtypeStruct((1,) + square, F32),
            jax.ShapeDtypeStruct((ROWS, 256 * SIDE), BF16),
        ),
        in_specs=[any_space] * 6,
        out_specs=(vmem, vmem, vmem),
        scratch_shapes=[
            pltpu.VMEM((8, 32), jnp.int32),
            pltpu.SMEM((8, 32), jnp.int32),
            pltpu.VMEM((8, 32), jnp.int32),
            pltpu.SMEM((8, 32), jnp.int32),
            pltpu.VMEM((ROWS, 256 * SIDE), BF16),
            pltpu.VMEM(square, BF16),
            pltpu.VMEM(square, BF16),
            pltpu.VMEM(square, F32),
            pltpu.VMEM(square, F32),
            pltpu.VMEM((16, 8) + blk, BF16),
            pltpu.VMEM((16, 8) + blk, BF16),
            pltpu.VMEM((16, 4) + blk, BF16),
            pltpu.VMEM((16, 4) + blk, BF16),
            pltpu.VMEM((16, 4) + blk, BF16),
            pltpu.VMEM((16, 4) + blk, BF16),
            pltpu.VMEM((2 * SIDE, SIDE), BF16),
            pltpu.VMEM(square, BF16),
            pltpu.VMEM(square, BF16),
            pltpu.VMEM(square, F32),
            pltpu.VMEM(square, BF16),
            pltpu.VMEM((16, 2, 2, 4) + blk, BF16),
            dma((3,)), dma, dma((2,)), dma((2,)), dma, dma((16,)), dma, dma((16, 4)), dma, dma,
            dma, dma((16, 4)), dma, dma((16,)), dma, dma((16,)),
            pltpu.SemaphoreType.REGULAR, pltpu.SemaphoreType.REGULAR, pltpu.SemaphoreType.REGULAR,
        ],
        compiler_params=pltpu.CompilerParams(
            collective_id=0, has_side_effects=True, vmem_limit_bytes=VMEM_MIB * 1024 * 1024
        ),
    )(*held)


def store_kernel(left_ref, right_ref, update_ref, left_out, right_out, update_out, sems):
    copies = [
        pltpu.make_async_copy(left_ref, left_out, sems.at[0]),
        pltpu.make_async_copy(right_ref, right_out, sems.at[1]),
    ]
    width = 256 * SIDE // 4
    for q in range(4):
        lanes = pl.ds(q * width, width)
        copies.append(
            pltpu.make_async_copy(update_ref.at[:, lanes], update_out.at[:, lanes], sems.at[2 + q])
        )
    for copy in copies:
        copy.start()
    for copy in copies:
        copy.wait()


def store(*arrays):
    any_space = pl.BlockSpec(memory_space=pl.ANY)
    held = [pltpu.with_memory_space_constraint(v, pltpu.VMEM) for v in arrays]
    return pl.pallas_call(
        store_kernel,
        out_shape=tuple(jax.ShapeDtypeStruct(v.shape, v.dtype) for v in arrays),
        in_specs=[any_space] * 3,
        out_specs=(any_space,) * 3,
        scratch_shapes=[pltpu.SemaphoreType.DMA((6,))],
        compiler_params=pltpu.CompilerParams(vmem_limit_bytes=16 * 1024 * 1024),
    )(*held)


def body(grad, owner_rep, stat_left, stat_right, root_left, root_right):
    done = exchange(owner_rep, grad, root_left, root_right, stat_left, stat_right)
    return store(*done)


def solution(mesh):
    owned = P(("rep", "shard"), None, None)
    return jax.shard_map(
        body,
        mesh=mesh,
        in_specs=(P("rep", "shard", None), P(), owned, owned, owned, owned),
        out_specs=(owned, owned, P("shard", None)),
        check_vma=False,
    )
```

```python
import jax
import jax.numpy as jnp
from jax import lax
from jax.experimental import pallas as pl
from jax.experimental.pallas import tpu as pltpu
from jax.sharding import PartitionSpec as P

MESH = pl.DeviceIdType.MESH
decay_rate = 0.9
ROWS = 16
SIDE = 512
GATE = 17
LAG = 5
WINDOW = 6
TRAIL = 4
FAR = (3, 2, 1, 0)
VMEM_MIB = 40
F32 = jnp.float32
BF16 = jnp.bfloat16


def rem(a, b):
    return lax.rem(a, jnp.int32(b))


def div(a, b):
    return lax.div(a, jnp.int32(b))


def exchange_kernel(
    own_ref, grad_ref, rl_ref, rr_ref, left_ref, right_ref,
    new_left_ref, new_right_ref, update_ref,
    own_v, own_s, inv_v, inv_s, first_v, grad_v, rl_v, rr_v, left_v, right_v,
    cs, cr, zs, zr, kp, ds, dr, g_v, half_v, pre_v, u_v, av,
    own_sem, load_sem, root_sem, stat_sem, cs_sem, cr_sem, zs_sem, zr_sem, ds_sem, dr_sem,
    us_sem, ur_sem, fs_sem, fr_sem, hs_sem, hr_sem, plane_sem, block_sem, gate_sem,
):
    rep = lax.axis_index("rep")
    s = lax.axis_index("shard")
    l, c = div(rep, 2), rem(rep, 2)
    x, h, y = div(s, 8), rem(div(s, 4), 2), rem(s, 4)
    z = h * 4 + l
    sgn = 2 * rem(l, 2) - 1
    rep_core = l * 2 + (1 - c)
    rep_pair = (l - sgn) * 2 + c

    slot_load = pltpu.make_async_copy(own_ref, own_s, own_sem.at[1])
    slot_load.start()
    own_load = pltpu.make_async_copy(own_ref, own_v, own_sem.at[0])
    own_load.start()
    width = 32 * SIDE * 2

    def load_part(step, target):
        lanes = pl.ds(pl.multiple_of(rem(x + step, 4) * width, width), width)
        return pltpu.make_async_copy(grad_ref.at[0, :, lanes], target, load_sem.at[step])

    loads = [load_part(0, first_v)] + [load_part(q, grad_v.at[q - 1]) for q in range(1, 4)]
    for load in loads:
        load.start()
    later = [
        pltpu.make_async_copy(rl_ref.at[0], rl_v, root_sem.at[0]),
        pltpu.make_async_copy(rr_ref.at[0], rr_v, root_sem.at[1]),
        pltpu.make_async_copy(left_ref.at[0], left_v, stat_sem.at[0]),
        pltpu.make_async_copy(right_ref.at[0], right_v, stat_sem.at[1]),
    ]

    def ring_z(offset):
        return rem(z + sgn * offset + 8, 8)

    def toward(m):
        return rem(x + div(m, 4), 4), rem(y + rem(m, 4), 4)

    def fro(m):
        return rem(x + 4 - div(m, 4), 4), rem(y + 4 - rem(m, 4), 4)

    def place(x2, y2, z2):
        return x2 * 8 + div(z2, 4) * 4 + y2

    def to(z2, x2, y2):
        return (rem(z2, 4) * 2 + c, place(x2, y2, z2))

    barrier = pltpu.get_barrier_semaphore()

    def greet(sem, device):
        pl.semaphore_signal(sem, inc=1, device_id=device, device_id_type=MESH)

    greet(barrier, (rep_core, s))
    for offset in (-1, 1, 2, 3, -2):
        greet(barrier, to(ring_z(offset), x, y))
    for step in (1, 2, 3):
        greet(barrier, to(z, rem(x + step, 4), y))
        greet(barrier, to(z, x, rem(y + step, 4)))

    own_load.wait()
    owners = own_v[...]
    lines = []
    for r in range(8):
        line = jnp.zeros((1, 32), jnp.int32)
        for k in range(1, 8):
            line = jnp.where(owners[k:k + 1] == r, k, line)
        lines.append(line)
    inv_v[...] = jnp.concatenate(lines, axis=0)
    inv_load = pltpu.make_async_copy(inv_v, inv_s, own_sem.at[2])
    inv_load.start()

    def block_of(m, early, x2, y2, z2, core):
        s2 = place(x2, y2, z2)
        owner = rem(z2, 4) * 2 + core
        at = (div(z2, 4) * 4 + y2) * 8
        if early:
            slot = jnp.int32(0)
            for k in range(1, 8):
                slot = jnp.where(own_s[k, s2] == owner, k, slot)
            return first_v[:, pl.ds((at + slot) * SIDE, SIDE)]
        slot = inv_s[owner, s2]
        return grad_v[div(m, 4) - 1, :, pl.ds((at + slot) * SIDE, SIDE)]

    def by_part(m, work):
        pl.when(m < 4)(lambda: work(True))
        pl.when(m >= 4)(lambda: work(False))

    offsets = (0, 1, 2, 3, -1, -2, -3, -4)

    def remote(src, dst, send, recv, device):
        return pltpu.make_async_remote_copy(
            src_ref=src, dst_ref=dst, send_sem=send, recv_sem=recv,
            device_id=device, device_id_type=MESH,
        )

    def drain(ref, sem):
        pltpu.make_async_copy(ref, ref, sem).wait()

    slot_load.wait()
    loads[0].wait()
    pl.semaphore_wait(barrier, 12)
    for step in (1, 2, 3):
        greet(plane_sem, to(z, x, rem(y + step, 4)))

    def core_step(m):
        x2, y2 = toward(m)

        def fill(early):
            for e in range(8):
                cs[m, e] = block_of(m, early, x2, y2, ring_z(offsets[e]), 1 - c)

        by_part(m, fill)
        remote(cs.at[m], cr.at[m], cs_sem, cr_sem.at[m], (rep_core, s)).start()

    def pair_step(m):
        x2, y2 = toward(m)
        drain(cr.at[m], cr_sem.at[m])

        def fill(early):
            for i in FAR:
                zs[m, i] = cr[m, i + 4] + block_of(m, early, x2, y2, ring_z(offsets[i + 4]), c)
                remote(zs.at[m, i], zr.at[m, i], zs_sem, zr_sem.at[m, i], (rep_pair, s)).start()
            for e in range(4):
                kp[m, e] = cr[m, e] + block_of(m, early, x2, y2, ring_z(offsets[e]), c)

        by_part(m, fill)

    def rest_loaded():
        inv_load.wait()
        for load in loads[1:]:
            load.wait()

    row = div(l, 2) * SIDE + s * ROWS

    def owner_step(m):
        x2, y2 = toward(m)
        target = dr.at[pl.ds(pl.multiple_of(row, ROWS), ROWS)]
        for i in FAR:
            drain(zr.at[m, i], zr_sem.at[m, i])
            ds[m, i] = zr[m, i] + kp[m, i]

            def send():
                remote(ds.at[m, i], target, ds_sem, dr_sem, to(ring_z(i), x2, y2)).start()

            if i == 0:
                @pl.when(m == 0)
                def _():
                    pltpu.make_async_copy(ds.at[m, i], target, dr_sem).start()

                pl.when(m > 0)(send)
            else:
                send()

    def feed(m, carry):
        pl.when(m == 4)(rest_loaded)
        core_step(m)
        return carry

    def collect_step(t, carry):
        pl.when((t == 4) & (c == 0))(rest_loaded)

        @pl.when(t < 16)
        def _():
            pair_step(t)

        @pl.when(t == 0)
        def _():
            pl.semaphore_wait(plane_sem, 3)
            for offset in (1, 2, 3, -2):
                greet(block_sem, to(ring_z(offset), x, y))

        @pl.when(t == LAG)
        def _():
            pl.semaphore_wait(block_sem, 4)

        @pl.when(t >= LAG)
        def _():
            owner_step(t - LAG)

        @pl.when((t >= LAG) & (c == 0))
        def _():
            core_step(t - LAG)

        @pl.when((t == GATE) & (c == 0))
        def _():
            greet(gate_sem, (rep_core, s))
        return carry

    lax.fori_loop(0, 16 * c, feed, 0)
    for copy in later:
        copy.start()

    @pl.when(c == 1)
    def _():
        pl.semaphore_wait(gate_sem, 1)

    lax.fori_loop(0, 16 + LAG, collect_step, 0)

    for copy in later:
        copy.wait()
    drain(dr, dr_sem)

    part = SIDE // 4

    def half_step(t, total):
        rows = pl.ds(pl.multiple_of(t * part, part), part)
        more = pl.ds(pl.multiple_of(SIDE + t * part, part), part)
        block = dr[rows, :].astype(F32) + dr[more, :].astype(F32)
        rounded = block.astype(BF16)
        g_v[rows, :] = rounded
        half = jnp.dot(rounded, rr_v[...], preferred_element_type=F32)
        half_v[rows, :] = half.astype(BF16)
        return total + jnp.sum((block * block).reshape(part // 8, 8, SIDE), axis=0)

    zero = jnp.zeros((8, SIDE), F32)
    total_g = lax.fori_loop(0, 4, half_step, zero)

    def pre_step(t, total):
        rows = pl.ds(pl.multiple_of(t * part, part), part)
        pre = jnp.dot(rl_v[rows, :], half_v[...], preferred_element_type=F32)
        pre_v[rows, :] = pre
        return total + jnp.sum((pre * pre).reshape(part // 8, 8, SIDE), axis=0)

    total_p = lax.fori_loop(0, 4, pre_step, zero)
    scale = jnp.sqrt(
        jnp.sum(total_g, keepdims=True) / (jnp.sum(total_p, keepdims=True) + 1e-06)
    )

    def scale_step(t, carry):
        rows = pl.ds(pl.multiple_of(t * part, part), part)
        u_v[rows, :] = (-(scale * pre_v[rows, :])).astype(BF16)
        return carry

    lax.fori_loop(0, 4, scale_step, 0)

    def spread(m):
        x2, y2 = toward(m)
        for i in range(4):
            z2 = ring_z(-i if i % 2 == 0 else i)
            device = to(z2, x2, y2)
            source = u_v.at[pl.ds(pl.multiple_of(device[1] * ROWS, ROWS), ROWS)]

            def send():
                remote(source, av.at[m, h, c, l], us_sem, ur_sem.at[m, i], device).start()

            if i == 0:
                @pl.when(m == 0)
                def _():
                    pltpu.make_async_copy(source, av.at[m, h, c, l], ur_sem.at[m, i]).start()

                pl.when(m > 0)(send)
            else:
                send()

    def forward_pair(m):
        for i in range(4):
            d = ring_z(i)
            slot = av.at[m, div(d, 4), c, rem(d, 4)]
            drain(slot, ur_sem.at[m, i])
            remote(slot, slot, fs_sem, fr_sem.at[m], (rep_pair, s)).start()

    def forward_core(m):
        drain(av.at[m, 0, c], fr_sem.at[m])
        for i in range(2):
            slot = av.at[m, i, c]
            remote(slot, slot, hs_sem, hr_sem.at[m], (rep_core, s)).start()

    def arrange(m):
        x1, y1 = fro(m)
        drain(av.at[m, 0], hr_sem.at[m])
        for i in range(2):
            s1 = x1 * 8 + i * 4 + y1
            slots = [own_s[k, s1] for k in range(8)]
            for q in range(4):
                lanes = pl.ds(q * 128, 128)
                pieces = [av[m, i, r % 2, r // 2, :, lanes] for r in range(8)]
                for k in range(8):
                    piece = pieces[0]
                    for r in range(1, 8):
                        piece = jnp.where(slots[k] == r, pieces[r], piece)
                    at = pl.multiple_of((s1 * 8 + k) * SIDE + q * 128, 128)
                    update_ref[:, pl.ds(at, 128)] = piece

    factor = (1.0 - decay_rate) / SIDE

    def stats(t):
        rows = pl.ds(pl.multiple_of(t * part, part), part)
        outer = lax.dot_general(
            g_v[rows, :], g_v[...], (((1,), (1,)), ((), ())), preferred_element_type=F32
        )
        new_left_ref[0, rows, :] = decay_rate * left_v[rows, :] + factor * outer
        inner = lax.dot_general(
            g_v[:, rows], g_v[...], (((0,), (0,)), ((), ())), preferred_element_type=F32
        )
        new_right_ref[0, rows, :] = decay_rate * right_v[rows, :] + factor * inner

    def spread_step(t, carry):
        @pl.when(t < 16)
        def _():
            spread(t)

        @pl.when((t >= WINDOW) & (t < 16 + WINDOW))
        def _():
            forward_pair(t - WINDOW)

        @pl.when((t >= WINDOW + TRAIL) & (t < 16 + WINDOW + TRAIL))
        def _():
            forward_core(t - WINDOW - TRAIL)

        @pl.when((t >= WINDOW + 2) & (t < WINDOW + 6))
        def _():
            stats(t - WINDOW - 2)

        @pl.when((t >= WINDOW + TRAIL + 1) & (c == 1))
        def _():
            arrange(t - WINDOW - TRAIL - 1)
        return carry

    def arrange_step(m, carry):
        arrange(m)
        return carry

    lax.fori_loop(0, 17 + WINDOW + TRAIL, spread_step, 0)
    lax.fori_loop(0, 16 * (1 - c), arrange_step, 0)

    drain(cs, cs_sem)
    drain(zs, zs_sem)
    drain(dr.at[pl.ds(0, 63 * ROWS)], ds_sem)
    drain(dr.at[pl.ds(0, 63 * ROWS)], us_sem)
    drain(zs, fs_sem)
    drain(zs, hs_sem)
    drain(zs, hs_sem)


def exchange(owner_rep, grad, root_left, root_right, stat_left, stat_right):
    held = [
        pltpu.with_memory_space_constraint(v, pltpu.HBM)
        for v in (owner_rep.T, grad, root_left, root_right, stat_left, stat_right)
    ]
    any_space = pl.BlockSpec(memory_space=pl.ANY)
    vmem = pl.BlockSpec(memory_space=pltpu.VMEM)
    dma = pltpu.SemaphoreType.DMA
    blk = (ROWS, SIDE)
    square = (SIDE, SIDE)
    return pl.pallas_call(
        exchange_kernel,
        out_shape=(
            jax.ShapeDtypeStruct((1,) + square, F32),
            jax.ShapeDtypeStruct((1,) + square, F32),
            jax.ShapeDtypeStruct((ROWS, 256 * SIDE), BF16),
        ),
        in_specs=[any_space] * 6,
        out_specs=(vmem, vmem, vmem),
        scratch_shapes=[
            pltpu.VMEM((8, 32), jnp.int32),
            pltpu.SMEM((8, 32), jnp.int32),
            pltpu.VMEM((8, 32), jnp.int32),
            pltpu.SMEM((8, 32), jnp.int32),
            pltpu.VMEM((ROWS, 64 * SIDE), BF16),
            pltpu.VMEM((3, ROWS, 64 * SIDE), BF16),
            pltpu.VMEM(square, BF16),
            pltpu.VMEM(square, BF16),
            pltpu.VMEM(square, F32),
            pltpu.VMEM(square, F32),
            pltpu.VMEM((16, 8) + blk, BF16),
            pltpu.VMEM((16, 8) + blk, BF16),
            pltpu.VMEM((16, 4) + blk, BF16),
            pltpu.VMEM((16, 4) + blk, BF16),
            pltpu.VMEM((16, 4) + blk, BF16),
            pltpu.VMEM((16, 4) + blk, BF16),
            pltpu.VMEM((2 * SIDE, SIDE), BF16),
            pltpu.VMEM(square, BF16),
            pltpu.VMEM(square, BF16),
            pltpu.VMEM(square, F32),
            pltpu.VMEM(square, BF16),
            pltpu.VMEM((16, 2, 2, 4) + blk, BF16),
            dma((3,)), dma((4,)), dma((2,)), dma((2,)), dma, dma((16,)), dma, dma((16, 4)), dma, dma,
            dma, dma((16, 4)), dma, dma((16,)), dma, dma((16,)),
            pltpu.SemaphoreType.REGULAR, pltpu.SemaphoreType.REGULAR, pltpu.SemaphoreType.REGULAR,
        ],
        compiler_params=pltpu.CompilerParams(
            collective_id=0, has_side_effects=True, vmem_limit_bytes=VMEM_MIB * 1024 * 1024
        ),
    )(*held)


def store_kernel(left_ref, right_ref, update_ref, left_out, right_out, update_out, sems):
    copies = [
        pltpu.make_async_copy(left_ref, left_out, sems.at[0]),
        pltpu.make_async_copy(right_ref, right_out, sems.at[1]),
    ]
    width = 256 * SIDE // 4
    for q in range(4):
        lanes = pl.ds(q * width, width)
        copies.append(
            pltpu.make_async_copy(update_ref.at[:, lanes], update_out.at[:, lanes], sems.at[2 + q])
        )
    for copy in copies:
        copy.start()
    for copy in copies:
        copy.wait()


def store(*arrays):
    any_space = pl.BlockSpec(memory_space=pl.ANY)
    held = [pltpu.with_memory_space_constraint(v, pltpu.VMEM) for v in arrays]
    return pl.pallas_call(
        store_kernel,
        out_shape=tuple(jax.ShapeDtypeStruct(v.shape, v.dtype) for v in arrays),
        in_specs=[any_space] * 3,
        out_specs=(any_space,) * 3,
        scratch_shapes=[pltpu.SemaphoreType.DMA((6,))],
        compiler_params=pltpu.CompilerParams(vmem_limit_bytes=16 * 1024 * 1024),
    )(*held)


def body(grad, owner_rep, stat_left, stat_right, root_left, root_right):
    done = exchange(owner_rep, grad, root_left, root_right, stat_left, stat_right)
    return store(*done)


def solution(mesh):
    owned = P(("rep", "shard"), None, None)
    return jax.shard_map(
        body,
        mesh=mesh,
        in_specs=(P("rep", "shard", None), P(), owned, owned, owned, owned),
        out_specs=(owned, owned, P("shard", None)),
        check_vma=False,
    )
```

```python
import jax
import jax.numpy as jnp
from jax import lax
from jax.experimental import pallas as pl
from jax.experimental.pallas import tpu as pltpu
from jax.sharding import PartitionSpec as P

MESH = pl.DeviceIdType.MESH
decay_rate = 0.9
ROWS = 16
SIDE = 512
GATE = 16
LAG = 5
WINDOW = 6
TRAIL = 4
FAR = (3, 2, 1, 0)
VMEM_MIB = 40
F32 = jnp.float32
BF16 = jnp.bfloat16


def rem(a, b):
    return lax.rem(a, jnp.int32(b))


def div(a, b):
    return lax.div(a, jnp.int32(b))


def exchange_kernel(
    own_ref, grad_ref, rl_ref, rr_ref, left_ref, right_ref,
    new_left_ref, new_right_ref, update_ref,
    own_v, own_s, inv_v, inv_s, first_v, grad_v, rl_v, rr_v, left_v, right_v,
    cs, cr, zs, zr, kp, ds, dr, g_v, half_v, pre_v, u_v, av,
    own_sem, load_sem, root_sem, stat_sem, cs_sem, cr_sem, zs_sem, zr_sem, ds_sem, dr_sem,
    us_sem, ur_sem, fs_sem, fr_sem, hs_sem, hr_sem, plane_sem, block_sem, gate_sem,
):
    rep = lax.axis_index("rep")
    s = lax.axis_index("shard")
    l, c = div(rep, 2), rem(rep, 2)
    x, h, y = div(s, 8), rem(div(s, 4), 2), rem(s, 4)
    z = h * 4 + l
    sgn = 2 * rem(l, 2) - 1
    rep_core = l * 2 + (1 - c)
    rep_pair = (l - sgn) * 2 + c

    later = [
        pltpu.make_async_copy(rl_ref.at[0], rl_v, root_sem.at[0]),
        pltpu.make_async_copy(rr_ref.at[0], rr_v, root_sem.at[1]),
        pltpu.make_async_copy(left_ref.at[0], left_v, stat_sem.at[0]),
        pltpu.make_async_copy(right_ref.at[0], right_v, stat_sem.at[1]),
    ]

    def ring_z(offset):
        return rem(z + sgn * offset + 8, 8)

    def shift(m):
        late = div(m + 12, 16)
        q = (m - 4) * late
        dx = late * (1 + rem(q, 3))
        dy = (1 - late) * m + late * rem(div(q, 3) + rem(q, 3), 4)
        return dx, dy

    def toward(m):
        dx, dy = shift(m)
        return rem(x + dx, 4), rem(y + dy, 4)

    def fro(m):
        dx, dy = shift(m)
        return rem(x + 4 - dx, 4), rem(y + 4 - dy, 4)

    def place(x2, y2, z2):
        return x2 * 8 + div(z2, 4) * 4 + y2

    def to(z2, x2, y2):
        return (rem(z2, 4) * 2 + c, place(x2, y2, z2))

    barrier = pltpu.get_barrier_semaphore()

    def greet(sem, device):
        pl.semaphore_signal(sem, inc=1, device_id=device, device_id_type=MESH)

    slot_load = pltpu.make_async_copy(own_ref, own_s, own_sem.at[1])
    slot_load.start()
    width = 32 * SIDE * 2

    def load_part(step, target):
        lanes = pl.ds(pl.multiple_of(rem(x + step, 4) * width, width), width)
        return pltpu.make_async_copy(grad_ref.at[0, :, lanes], target, load_sem.at[step])

    loads = [load_part(0, first_v)] + [load_part(q, grad_v.at[q - 1]) for q in range(1, 4)]
    loads[0].start()
    greet(barrier, (rep_core, s))
    for offset in (-1, 1, 2, 3, -2):
        greet(barrier, to(ring_z(offset), x, y))
    for step in (1, 2, 3):
        greet(barrier, to(z, rem(x + step, 4), y))
        greet(barrier, to(z, x, rem(y + step, 4)))

    for load in loads[1:]:
        load.start()
    own_load = pltpu.make_async_copy(own_ref, own_v, own_sem.at[0])
    own_load.start()

    def block_of(m, early, x2, y2, z2, core):
        s2 = place(x2, y2, z2)
        owner = rem(z2, 4) * 2 + core
        at = (div(z2, 4) * 4 + y2) * 8
        if early:
            slot = jnp.int32(0)
            for k in range(1, 8):
                slot = jnp.where(own_s[k, s2] == owner, k, slot)
            return first_v[:, pl.ds((at + slot) * SIDE, SIDE)]
        slot = inv_s[owner, s2]
        return grad_v[shift(m)[0] - 1, :, pl.ds((at + slot) * SIDE, SIDE)]

    def by_part(m, work):
        pl.when(m < 4)(lambda: work(True))
        pl.when(m >= 4)(lambda: work(False))

    offsets = (0, 1, 2, 3, -1, -2, -3, -4)

    def remote(src, dst, send, recv, device):
        return pltpu.make_async_remote_copy(
            src_ref=src, dst_ref=dst, send_sem=send, recv_sem=recv,
            device_id=device, device_id_type=MESH,
        )

    def drain(ref, sem):
        pltpu.make_async_copy(ref, ref, sem).wait()

    slot_load.wait()
    loads[0].wait()
    pl.semaphore_wait(barrier, 12)
    for step in (1, 2, 3):
        greet(plane_sem, to(z, x, rem(y + step, 4)))

    def core_step(m):
        x2, y2 = toward(m)

        def fill(early):
            for e in range(8):
                cs[m, e] = block_of(m, early, x2, y2, ring_z(offsets[e]), 1 - c)

        by_part(m, fill)
        remote(cs.at[m], cr.at[m], cs_sem, cr_sem.at[m], (rep_core, s)).start()

    def pair_step(m):
        x2, y2 = toward(m)
        drain(cr.at[m], cr_sem.at[m])

        def fill(early):
            for i in FAR:
                zs[m, i] = cr[m, i + 4] + block_of(m, early, x2, y2, ring_z(offsets[i + 4]), c)
                remote(zs.at[m, i], zr.at[m, i], zs_sem, zr_sem.at[m, i], (rep_pair, s)).start()
            for e in range(4):
                kp[m, e] = cr[m, e] + block_of(m, early, x2, y2, ring_z(offsets[e]), c)

        by_part(m, fill)

    def rest_loaded():
        own_load.wait()
        owners = own_v[...]
        lines = []
        for r in range(8):
            line = jnp.zeros((1, 32), jnp.int32)
            for k in range(1, 8):
                line = jnp.where(owners[k:k + 1] == r, k, line)
            lines.append(line)
        inv_v[...] = jnp.concatenate(lines, axis=0)
        inv_load = pltpu.make_async_copy(inv_v, inv_s, own_sem.at[2])
        inv_load.start()
        inv_load.wait()
        for load in loads[1:]:
            load.wait()

    row = div(l, 2) * SIDE + s * ROWS

    def owner_step(m):
        x2, y2 = toward(m)
        target = dr.at[pl.ds(pl.multiple_of(row, ROWS), ROWS)]
        for i in FAR:
            drain(zr.at[m, i], zr_sem.at[m, i])
            ds[m, i] = zr[m, i] + kp[m, i]

            def send():
                remote(ds.at[m, i], target, ds_sem, dr_sem, to(ring_z(i), x2, y2)).start()

            if i == 0:
                @pl.when(m == 0)
                def _():
                    pltpu.make_async_copy(ds.at[m, i], target, dr_sem).start()

                pl.when(m > 0)(send)
            else:
                send()

    def feed(m, carry):
        pl.when(m == 4)(rest_loaded)
        core_step(m)
        return carry

    def collect_step(t, carry):
        pl.when((t == 4) & (c == 0))(rest_loaded)

        @pl.when(t < 16)
        def _():
            pair_step(t)

        @pl.when(t == 0)
        def _():
            pl.semaphore_wait(plane_sem, 3)
            for offset in (1, 2, 3, -2):
                greet(block_sem, to(ring_z(offset), x, y))

        @pl.when(t == LAG)
        def _():
            pl.semaphore_wait(block_sem, 4)

        @pl.when(t >= LAG)
        def _():
            owner_step(t - LAG)

        @pl.when((t >= LAG) & (c == 0))
        def _():
            core_step(t - LAG)

        @pl.when((t == GATE) & (c == 0))
        def _():
            greet(gate_sem, (rep_core, s))
        return carry

    lax.fori_loop(0, 16 * c, feed, 0)
    for copy in later:
        copy.start()

    @pl.when(c == 1)
    def _():
        pl.semaphore_wait(gate_sem, 1)

    lax.fori_loop(0, 16 + LAG, collect_step, 0)

    for copy in later:
        copy.wait()
    drain(dr, dr_sem)

    part = SIDE // 4

    def half_step(t, total):
        rows = pl.ds(pl.multiple_of(t * part, part), part)
        more = pl.ds(pl.multiple_of(SIDE + t * part, part), part)
        block = dr[rows, :].astype(F32) + dr[more, :].astype(F32)
        rounded = block.astype(BF16)
        g_v[rows, :] = rounded
        half = jnp.dot(rounded, rr_v[...], preferred_element_type=F32)
        half_v[rows, :] = half.astype(BF16)
        return total + jnp.sum((block * block).reshape(part // 8, 8, SIDE), axis=0)

    zero = jnp.zeros((8, SIDE), F32)
    total_g = lax.fori_loop(0, 4, half_step, zero)

    def pre_step(t, total):
        rows = pl.ds(pl.multiple_of(t * part, part), part)
        pre = jnp.dot(rl_v[rows, :], half_v[...], preferred_element_type=F32)
        pre_v[rows, :] = pre
        return total + jnp.sum((pre * pre).reshape(part // 8, 8, SIDE), axis=0)

    total_p = lax.fori_loop(0, 4, pre_step, zero)
    scale = jnp.sqrt(
        jnp.sum(total_g, keepdims=True) / (jnp.sum(total_p, keepdims=True) + 1e-06)
    )

    def scale_step(t, carry):
        rows = pl.ds(pl.multiple_of(t * part, part), part)
        u_v[rows, :] = (-(scale * pre_v[rows, :])).astype(BF16)
        return carry

    lax.fori_loop(0, 4, scale_step, 0)

    def spread(m):
        x2, y2 = toward(m)
        for i in FAR:
            z2 = ring_z(-i if i % 2 == 0 else i)
            device = to(z2, x2, y2)
            source = u_v.at[pl.ds(pl.multiple_of(device[1] * ROWS, ROWS), ROWS)]

            def send():
                remote(source, av.at[m, h, c, l], us_sem, ur_sem.at[m, i], device).start()

            if i == 0:
                @pl.when(m == 0)
                def _():
                    pltpu.make_async_copy(source, av.at[m, h, c, l], ur_sem.at[m, i]).start()

                pl.when(m > 0)(send)
            else:
                send()

    def forward_pair(m):
        for i in FAR:
            d = ring_z(i)
            slot = av.at[m, div(d, 4), c, rem(d, 4)]
            drain(slot, ur_sem.at[m, i])
            remote(slot, slot, fs_sem, fr_sem.at[m], (rep_pair, s)).start()

    def forward_core(m):
        drain(av.at[m, 0, c], fr_sem.at[m])
        for i in range(2):
            slot = av.at[m, i, c]
            remote(slot, slot, hs_sem, hr_sem.at[m], (rep_core, s)).start()

    def arrange(m):
        x1, y1 = fro(m)
        drain(av.at[m, 0], hr_sem.at[m])
        for i in range(2):
            s1 = x1 * 8 + i * 4 + y1
            slots = [own_s[k, s1] for k in range(8)]
            for q in range(4):
                lanes = pl.ds(q * 128, 128)
                pieces = [av[m, i, r % 2, r // 2, :, lanes] for r in range(8)]
                for k in range(8):
                    piece = pieces[0]
                    for r in range(1, 8):
                        piece = jnp.where(slots[k] == r, pieces[r], piece)
                    at = pl.multiple_of((s1 * 8 + k) * SIDE + q * 128, 128)
                    update_ref[:, pl.ds(at, 128)] = piece

    factor = (1.0 - decay_rate) / SIDE

    def stats(t):
        rows = pl.ds(pl.multiple_of(t * part, part), part)
        outer = lax.dot_general(
            g_v[rows, :], g_v[...], (((1,), (1,)), ((), ())), preferred_element_type=F32
        )
        new_left_ref[0, rows, :] = decay_rate * left_v[rows, :] + factor * outer
        inner = lax.dot_general(
            g_v[:, rows], g_v[...], (((0,), (0,)), ((), ())), preferred_element_type=F32
        )
        new_right_ref[0, rows, :] = decay_rate * right_v[rows, :] + factor * inner

    def spread_step(t, carry):
        @pl.when(t < 16)
        def _():
            spread(t)

        @pl.when((t >= WINDOW) & (t < 16 + WINDOW))
        def _():
            forward_pair(t - WINDOW)

        @pl.when((t >= WINDOW + TRAIL) & (t < 16 + WINDOW + TRAIL))
        def _():
            forward_core(t - WINDOW - TRAIL)

        @pl.when((t >= WINDOW + 2) & (t < WINDOW + 6))
        def _():
            stats(t - WINDOW - 2)

        @pl.when((t >= WINDOW + TRAIL + 1) & (c == 1))
        def _():
            arrange(t - WINDOW - TRAIL - 1)
        return carry

    def arrange_step(m, carry):
        arrange(m)
        return carry

    lax.fori_loop(0, 17 + WINDOW + TRAIL, spread_step, 0)
    drain(cs, cs_sem)
    drain(zs, zs_sem)
    drain(dr.at[pl.ds(0, 63 * ROWS)], ds_sem)
    drain(dr.at[pl.ds(0, 63 * ROWS)], us_sem)
    drain(zs, fs_sem)
    drain(zs, hs_sem)
    drain(zs, hs_sem)
    lax.fori_loop(0, 16 * (1 - c), arrange_step, 0)


def exchange(owner_rep, grad, root_left, root_right, stat_left, stat_right):
    held = [
        pltpu.with_memory_space_constraint(v, pltpu.HBM)
        for v in (owner_rep.T, grad, root_left, root_right, stat_left, stat_right)
    ]
    any_space = pl.BlockSpec(memory_space=pl.ANY)
    vmem = pl.BlockSpec(memory_space=pltpu.VMEM)
    dma = pltpu.SemaphoreType.DMA
    blk = (ROWS, SIDE)
    square = (SIDE, SIDE)
    return pl.pallas_call(
        exchange_kernel,
        out_shape=(
            jax.ShapeDtypeStruct((1,) + square, F32),
            jax.ShapeDtypeStruct((1,) + square, F32),
            jax.ShapeDtypeStruct((ROWS, 256 * SIDE), BF16),
        ),
        in_specs=[any_space] * 6,
        out_specs=(vmem, vmem, vmem),
        scratch_shapes=[
            pltpu.VMEM((8, 32), jnp.int32),
            pltpu.SMEM((8, 32), jnp.int32),
            pltpu.VMEM((8, 32), jnp.int32),
            pltpu.SMEM((8, 32), jnp.int32),
            pltpu.VMEM((ROWS, 64 * SIDE), BF16),
            pltpu.VMEM((3, ROWS, 64 * SIDE), BF16),
            pltpu.VMEM(square, BF16),
            pltpu.VMEM(square, BF16),
            pltpu.VMEM(square, F32),
            pltpu.VMEM(square, F32),
            pltpu.VMEM((16, 8) + blk, BF16),
            pltpu.VMEM((16, 8) + blk, BF16),
            pltpu.VMEM((16, 4) + blk, BF16),
            pltpu.VMEM((16, 4) + blk, BF16),
            pltpu.VMEM((16, 4) + blk, BF16),
            pltpu.VMEM((16, 4) + blk, BF16),
            pltpu.VMEM((2 * SIDE, SIDE), BF16),
            pltpu.VMEM(square, BF16),
            pltpu.VMEM(square, BF16),
            pltpu.VMEM(square, F32),
            pltpu.VMEM(square, BF16),
            pltpu.VMEM((16, 2, 2, 4) + blk, BF16),
            dma((3,)), dma((4,)), dma((2,)), dma((2,)), dma, dma((16,)), dma, dma((16, 4)), dma, dma,
            dma, dma((16, 4)), dma, dma((16,)), dma, dma((16,)),
            pltpu.SemaphoreType.REGULAR, pltpu.SemaphoreType.REGULAR, pltpu.SemaphoreType.REGULAR,
        ],
        compiler_params=pltpu.CompilerParams(
            collective_id=0, has_side_effects=True, vmem_limit_bytes=VMEM_MIB * 1024 * 1024
        ),
    )(*held)


def store_kernel(left_ref, right_ref, update_ref, left_out, right_out, update_out, sems):
    copies = [
        pltpu.make_async_copy(left_ref, left_out, sems.at[0]),
        pltpu.make_async_copy(right_ref, right_out, sems.at[1]),
    ]
    width = 256 * SIDE // 4
    for q in range(4):
        lanes = pl.ds(q * width, width)
        copies.append(
            pltpu.make_async_copy(update_ref.at[:, lanes], update_out.at[:, lanes], sems.at[2 + q])
        )
    for copy in copies:
        copy.start()
    for copy in copies:
        copy.wait()


def store(*arrays):
    any_space = pl.BlockSpec(memory_space=pl.ANY)
    held = [pltpu.with_memory_space_constraint(v, pltpu.VMEM) for v in arrays]
    return pl.pallas_call(
        store_kernel,
        out_shape=tuple(jax.ShapeDtypeStruct(v.shape, v.dtype) for v in arrays),
        in_specs=[any_space] * 3,
        out_specs=(any_space,) * 3,
        scratch_shapes=[pltpu.SemaphoreType.DMA((6,))],
        compiler_params=pltpu.CompilerParams(vmem_limit_bytes=16 * 1024 * 1024),
    )(*held)


def body(grad, owner_rep, stat_left, stat_right, root_left, root_right):
    done = exchange(owner_rep, grad, root_left, root_right, stat_left, stat_right)
    return store(*done)


def solution(mesh):
    owned = P(("rep", "shard"), None, None)
    return jax.shard_map(
        body,
        mesh=mesh,
        in_specs=(P("rep", "shard", None), P(), owned, owned, owned, owned),
        out_specs=(owned, owned, P("shard", None)),
        check_vma=False,
    )
```

```python
import jax
import jax.numpy as jnp
from jax import lax
from jax.experimental import pallas as pl
from jax.experimental.pallas import tpu as pltpu
from jax.sharding import PartitionSpec as P

MESH = pl.DeviceIdType.MESH
decay_rate = 0.9
ROWS = 16
SIDE = 512
GATE = 16
LAG = 5
WINDOW = 6
TRAIL = 4
FAR = (3, 2, 1, 0)
VMEM_MIB = 40
F32 = jnp.float32
BF16 = jnp.bfloat16


def rem(a, b):
    return lax.rem(a, jnp.int32(b))


def div(a, b):
    return lax.div(a, jnp.int32(b))


def exchange_kernel(
    own_ref, grad_ref, rl_ref, rr_ref, left_ref, right_ref,
    new_left_ref, new_right_ref, update_ref,
    own_v, own_s, inv_v, inv_s, first_v, grad_v, rl_v, rr_v, left_v, right_v,
    cs, cr, zs, zr, kp, ds, dr, g_v, pre_v, u_v, av,
    own_sem, load_sem, root_sem, stat_sem, cs_sem, cr_sem, zs_sem, zr_sem, ds_sem, dr_sem,
    us_sem, ur_sem, fs_sem, fr_sem, hs_sem, hr_sem, plane_sem, block_sem, gate_sem,
):
    rep = lax.axis_index("rep")
    s = lax.axis_index("shard")
    l, c = div(rep, 2), rem(rep, 2)
    x, h, y = div(s, 8), rem(div(s, 4), 2), rem(s, 4)
    z = h * 4 + l
    sgn = 2 * rem(l, 2) - 1
    rep_core = l * 2 + (1 - c)
    rep_pair = (l - sgn) * 2 + c

    later = [
        pltpu.make_async_copy(rl_ref.at[0], rl_v, root_sem.at[0]),
        pltpu.make_async_copy(rr_ref.at[0], rr_v, root_sem.at[1]),
        pltpu.make_async_copy(left_ref.at[0], left_v, stat_sem.at[0]),
        pltpu.make_async_copy(right_ref.at[0], right_v, stat_sem.at[1]),
    ]

    def ring_z(offset):
        return rem(z + sgn * offset + 8, 8)

    def shift(m):
        late = div(m + 12, 16)
        q = (m - 4) * late
        dx = late * (1 + rem(q, 3))
        dy = (1 - late) * m + late * rem(div(q, 3) + rem(q, 3), 4)
        return dx, dy

    def toward(m):
        dx, dy = shift(m)
        return rem(x + dx, 4), rem(y + dy, 4)

    def fro(m):
        dx, dy = shift(m)
        return rem(x + 4 - dx, 4), rem(y + 4 - dy, 4)

    def place(x2, y2, z2):
        return x2 * 8 + div(z2, 4) * 4 + y2

    def to(z2, x2, y2):
        return (rem(z2, 4) * 2 + c, place(x2, y2, z2))

    barrier = pltpu.get_barrier_semaphore()

    def greet(sem, device):
        pl.semaphore_signal(sem, inc=1, device_id=device, device_id_type=MESH)

    slot_load = pltpu.make_async_copy(own_ref, own_s, own_sem.at[1])
    slot_load.start()
    width = 32 * SIDE * 2

    def load_part(step, target):
        lanes = pl.ds(pl.multiple_of(rem(x + step, 4) * width, width), width)
        return pltpu.make_async_copy(grad_ref.at[0, :, lanes], target, load_sem.at[step])

    loads = [load_part(0, first_v)] + [load_part(q, grad_v.at[q - 1]) for q in range(1, 4)]
    loads[0].start()
    greet(barrier, (rep_core, s))
    for offset in (-1, 1, 2, 3, -2):
        greet(barrier, to(ring_z(offset), x, y))
    for step in (1, 2, 3):
        greet(barrier, to(z, rem(x + step, 4), y))
        greet(barrier, to(z, x, rem(y + step, 4)))

    for load in loads[1:]:
        load.start()
    own_load = pltpu.make_async_copy(own_ref, own_v, own_sem.at[0])
    own_load.start()

    def block_of(m, early, x2, y2, z2, core):
        s2 = place(x2, y2, z2)
        owner = rem(z2, 4) * 2 + core
        at = (div(z2, 4) * 4 + y2) * 8
        if early:
            slot = jnp.int32(0)
            for k in range(1, 8):
                slot = jnp.where(own_s[k, s2] == owner, k, slot)
            return first_v[:, pl.ds((at + slot) * SIDE, SIDE)]
        slot = inv_s[owner, s2]
        return grad_v[shift(m)[0] - 1, :, pl.ds((at + slot) * SIDE, SIDE)]

    def by_part(m, work):
        pl.when(m < 4)(lambda: work(True))
        pl.when(m >= 4)(lambda: work(False))

    offsets = (0, 1, 2, 3, -1, -2, -3, -4)

    def remote(src, dst, send, recv, device):
        return pltpu.make_async_remote_copy(
            src_ref=src, dst_ref=dst, send_sem=send, recv_sem=recv,
            device_id=device, device_id_type=MESH,
        )

    def drain(ref, sem):
        pltpu.make_async_copy(ref, ref, sem).wait()

    slot_load.wait()
    loads[0].wait()
    pl.semaphore_wait(barrier, 12)
    for step in (1, 2, 3):
        greet(plane_sem, to(z, x, rem(y + step, 4)))

    def core_step(m):
        x2, y2 = toward(m)

        def fill(early):
            for e in range(8):
                cs[m, e] = block_of(m, early, x2, y2, ring_z(offsets[e]), 1 - c)

        by_part(m, fill)
        remote(cs.at[m], cr.at[m], cs_sem, cr_sem.at[m], (rep_core, s)).start()

    def pair_step(m):
        x2, y2 = toward(m)
        drain(cr.at[m], cr_sem.at[m])

        def fill(early):
            for i in FAR:
                zs[m, i] = cr[m, i + 4] + block_of(m, early, x2, y2, ring_z(offsets[i + 4]), c)
                remote(zs.at[m, i], zr.at[m, i], zs_sem, zr_sem.at[m, i], (rep_pair, s)).start()
            for e in range(4):
                kp[m, e] = cr[m, e] + block_of(m, early, x2, y2, ring_z(offsets[e]), c)

        by_part(m, fill)

    def rest_loaded():
        own_load.wait()
        owners = own_v[...]
        lines = []
        for r in range(8):
            line = jnp.zeros((1, 32), jnp.int32)
            for k in range(1, 8):
                line = jnp.where(owners[k:k + 1] == r, k, line)
            lines.append(line)
        inv_v[...] = jnp.concatenate(lines, axis=0)
        inv_load = pltpu.make_async_copy(inv_v, inv_s, own_sem.at[2])
        inv_load.start()
        inv_load.wait()
        for load in loads[1:]:
            load.wait()

    row = div(l, 2) * SIDE + s * ROWS

    def owner_step(m):
        x2, y2 = toward(m)
        target = dr.at[pl.ds(pl.multiple_of(row, ROWS), ROWS)]
        for i in FAR:
            drain(zr.at[m, i], zr_sem.at[m, i])
            ds[m, i] = zr[m, i] + kp[m, i]

            def send():
                remote(ds.at[m, i], target, ds_sem, dr_sem.at[shift(m)[0]], to(ring_z(i), x2, y2)).start()

            if i == 0:
                @pl.when(m == 0)
                def _():
                    pltpu.make_async_copy(ds.at[m, i], target, dr_sem.at[0]).start()

                pl.when(m > 0)(send)
            else:
                send()

    def feed(m, carry):
        pl.when(m == 4)(rest_loaded)
        core_step(m)
        return carry

    def collect_step(t, carry):
        pl.when((t == 4) & (c == 0))(rest_loaded)

        @pl.when(t < 16)
        def _():
            pair_step(t)

        @pl.when(t == 0)
        def _():
            pl.semaphore_wait(plane_sem, 3)
            for offset in (1, 2, 3, -2):
                greet(block_sem, to(ring_z(offset), x, y))

        @pl.when(t == LAG)
        def _():
            pl.semaphore_wait(block_sem, 4)

        @pl.when(t >= LAG)
        def _():
            owner_step(t - LAG)

        @pl.when((t >= LAG) & (c == 0))
        def _():
            core_step(t - LAG)

        @pl.when((t == GATE) & (c == 0))
        def _():
            greet(gate_sem, (rep_core, s))
        return carry

    lax.fori_loop(0, 16 * c, feed, 0)
    for copy in later:
        copy.start()

    @pl.when(c == 1)
    def _():
        pl.semaphore_wait(gate_sem, 1)

    lax.fori_loop(0, 16 + LAG, collect_step, 0)

    for copy in later:
        copy.wait()
    part = SIDE // 4
    zero = jnp.zeros((8, SIDE), F32)

    def half_step(t, total):
        drain(dr.at[pl.ds(0, 2 * part)], dr_sem.at[t])
        at = pl.multiple_of(rem(x + 4 - t, 4) * part, part)
        rows = pl.ds(at, part)
        block = dr[rows, :].astype(F32) + dr[pl.ds(SIDE + at, part), :].astype(F32)
        rounded = block.astype(BF16)
        g_v[rows, :] = rounded
        half = jnp.dot(rounded, rr_v[...], preferred_element_type=F32).astype(BF16)
        pre = jnp.dot(rl_v[:, rows], half, preferred_element_type=F32)

        @pl.when(t == 0)
        def _():
            pre_v[...] = pre

        @pl.when(t > 0)
        def _():
            pre_v[...] = pre_v[...] + pre
        return total + jnp.sum((block * block).reshape(part // 8, 8, SIDE), axis=0)

    total_g = lax.fori_loop(0, 4, half_step, zero)

    def pre_step(t, total):
        rows = pl.ds(pl.multiple_of(t * part, part), part)
        pre = pre_v[rows, :]
        return total + jnp.sum((pre * pre).reshape(part // 8, 8, SIDE), axis=0)

    total_p = lax.fori_loop(0, 4, pre_step, zero)
    scale = jnp.sqrt(
        jnp.sum(total_g, keepdims=True) / (jnp.sum(total_p, keepdims=True) + 1e-06)
    )

    def scale_step(t, carry):
        rows = pl.ds(pl.multiple_of(t * part, part), part)
        u_v[rows, :] = (-(scale * pre_v[rows, :])).astype(BF16)
        return carry

    lax.fori_loop(0, 4, scale_step, 0)

    def spread(m):
        x2, y2 = toward(m)
        for i in FAR:
            z2 = ring_z(-i if i % 2 == 0 else i)
            device = to(z2, x2, y2)
            source = u_v.at[pl.ds(pl.multiple_of(device[1] * ROWS, ROWS), ROWS)]

            def send():
                remote(source, av.at[m, h, c, l], us_sem, ur_sem.at[m, i], device).start()

            if i == 0:
                @pl.when(m == 0)
                def _():
                    pltpu.make_async_copy(source, av.at[m, h, c, l], ur_sem.at[m, i]).start()

                pl.when(m > 0)(send)
            else:
                send()

    def forward_pair(m):
        for i in FAR:
            d = ring_z(i)
            slot = av.at[m, div(d, 4), c, rem(d, 4)]
            drain(slot, ur_sem.at[m, i])
            remote(slot, slot, fs_sem, fr_sem.at[m], (rep_pair, s)).start()

    def forward_core(m):
        drain(av.at[m, 0, c], fr_sem.at[m])
        for i in range(2):
            slot = av.at[m, i, c]
            remote(slot, slot, hs_sem, hr_sem.at[m], (rep_core, s)).start()

    def arrange(m):
        x1, y1 = fro(m)
        drain(av.at[m, 0], hr_sem.at[m])
        for i in range(2):
            s1 = x1 * 8 + i * 4 + y1
            slots = [own_s[k, s1] for k in range(8)]
            for q in range(4):
                lanes = pl.ds(q * 128, 128)
                pieces = [av[m, i, r % 2, r // 2, :, lanes] for r in range(8)]
                for k in range(8):
                    piece = pieces[0]
                    for r in range(1, 8):
                        piece = jnp.where(slots[k] == r, pieces[r], piece)
                    at = pl.multiple_of((s1 * 8 + k) * SIDE + q * 128, 128)
                    update_ref[:, pl.ds(at, 128)] = piece

    factor = (1.0 - decay_rate) / SIDE

    def stats(t):
        rows = pl.ds(pl.multiple_of(t * part, part), part)
        outer = lax.dot_general(
            g_v[rows, :], g_v[...], (((1,), (1,)), ((), ())), preferred_element_type=F32
        )
        new_left_ref[0, rows, :] = decay_rate * left_v[rows, :] + factor * outer
        inner = lax.dot_general(
            g_v[:, rows], g_v[...], (((0,), (0,)), ((), ())), preferred_element_type=F32
        )
        new_right_ref[0, rows, :] = decay_rate * right_v[rows, :] + factor * inner

    def spread_step(t, carry):
        @pl.when(t < 16)
        def _():
            spread(t)

        @pl.when((t >= WINDOW) & (t < 16 + WINDOW))
        def _():
            forward_pair(t - WINDOW)

        @pl.when((t >= WINDOW + TRAIL) & (t < 16 + WINDOW + TRAIL))
        def _():
            forward_core(t - WINDOW - TRAIL)

        @pl.when((t >= WINDOW + 2) & (t < WINDOW + 6))
        def _():
            stats(t - WINDOW - 2)

        @pl.when((t >= WINDOW + TRAIL + 1) & (c == 1))
        def _():
            arrange(t - WINDOW - TRAIL - 1)
        return carry

    def arrange_step(m, carry):
        arrange(m)
        return carry

    lax.fori_loop(0, 17 + WINDOW + TRAIL, spread_step, 0)
    drain(cs, cs_sem)
    drain(zs, zs_sem)
    drain(dr.at[pl.ds(0, 63 * ROWS)], ds_sem)
    drain(dr.at[pl.ds(0, 63 * ROWS)], us_sem)
    drain(zs, fs_sem)
    drain(zs, hs_sem)
    drain(zs, hs_sem)
    lax.fori_loop(0, 16 * (1 - c), arrange_step, 0)


def exchange(owner_rep, grad, root_left, root_right, stat_left, stat_right):
    held = [
        pltpu.with_memory_space_constraint(v, pltpu.HBM)
        for v in (owner_rep.T, grad, root_left, root_right, stat_left, stat_right)
    ]
    any_space = pl.BlockSpec(memory_space=pl.ANY)
    vmem = pl.BlockSpec(memory_space=pltpu.VMEM)
    dma = pltpu.SemaphoreType.DMA
    blk = (ROWS, SIDE)
    square = (SIDE, SIDE)
    return pl.pallas_call(
        exchange_kernel,
        out_shape=(
            jax.ShapeDtypeStruct((1,) + square, F32),
            jax.ShapeDtypeStruct((1,) + square, F32),
            jax.ShapeDtypeStruct((ROWS, 256 * SIDE), BF16),
        ),
        in_specs=[any_space] * 6,
        out_specs=(vmem, vmem, vmem),
        scratch_shapes=[
            pltpu.VMEM((8, 32), jnp.int32),
            pltpu.SMEM((8, 32), jnp.int32),
            pltpu.VMEM((8, 32), jnp.int32),
            pltpu.SMEM((8, 32), jnp.int32),
            pltpu.VMEM((ROWS, 64 * SIDE), BF16),
            pltpu.VMEM((3, ROWS, 64 * SIDE), BF16),
            pltpu.VMEM(square, BF16),
            pltpu.VMEM(square, BF16),
            pltpu.VMEM(square, F32),
            pltpu.VMEM(square, F32),
            pltpu.VMEM((16, 8) + blk, BF16),
            pltpu.VMEM((16, 8) + blk, BF16),
            pltpu.VMEM((16, 4) + blk, BF16),
            pltpu.VMEM((16, 4) + blk, BF16),
            pltpu.VMEM((16, 4) + blk, BF16),
            pltpu.VMEM((16, 4) + blk, BF16),
            pltpu.VMEM((2 * SIDE, SIDE), BF16),
            pltpu.VMEM(square, BF16),
            pltpu.VMEM(square, F32),
            pltpu.VMEM(square, BF16),
            pltpu.VMEM((16, 2, 2, 4) + blk, BF16),
            dma((3,)), dma((4,)), dma((2,)), dma((2,)), dma, dma((16,)), dma, dma((16, 4)), dma, dma((4,)),
            dma, dma((16, 4)), dma, dma((16,)), dma, dma((16,)),
            pltpu.SemaphoreType.REGULAR, pltpu.SemaphoreType.REGULAR, pltpu.SemaphoreType.REGULAR,
        ],
        compiler_params=pltpu.CompilerParams(
            collective_id=0, has_side_effects=True, vmem_limit_bytes=VMEM_MIB * 1024 * 1024
        ),
    )(*held)


def store_kernel(left_ref, right_ref, update_ref, left_out, right_out, update_out, sems):
    copies = [
        pltpu.make_async_copy(left_ref, left_out, sems.at[0]),
        pltpu.make_async_copy(right_ref, right_out, sems.at[1]),
    ]
    width = 256 * SIDE // 4
    for q in range(4):
        lanes = pl.ds(q * width, width)
        copies.append(
            pltpu.make_async_copy(update_ref.at[:, lanes], update_out.at[:, lanes], sems.at[2 + q])
        )
    for copy in copies:
        copy.start()
    for copy in copies:
        copy.wait()


def store(*arrays):
    any_space = pl.BlockSpec(memory_space=pl.ANY)
    held = [pltpu.with_memory_space_constraint(v, pltpu.VMEM) for v in arrays]
    return pl.pallas_call(
        store_kernel,
        out_shape=tuple(jax.ShapeDtypeStruct(v.shape, v.dtype) for v in arrays),
        in_specs=[any_space] * 3,
        out_specs=(any_space,) * 3,
        scratch_shapes=[pltpu.SemaphoreType.DMA((6,))],
        compiler_params=pltpu.CompilerParams(vmem_limit_bytes=16 * 1024 * 1024),
    )(*held)


def body(grad, owner_rep, stat_left, stat_right, root_left, root_right):
    done = exchange(owner_rep, grad, root_left, root_right, stat_left, stat_right)
    return store(*done)


def solution(mesh):
    owned = P(("rep", "shard"), None, None)
    return jax.shard_map(
        body,
        mesh=mesh,
        in_specs=(P("rep", "shard", None), P(), owned, owned, owned, owned),
        out_specs=(owned, owned, P("shard", None)),
        check_vma=False,
    )
```
